32 devices in a mesh: grid: 4 (over y, x), pair: 8 (over z, core).
Axes of the slice: x: 2, y: 2, z: 4, core: 2. Of those that a mesh axis runs over, the one named last changes fastest.
Arguments:
- amplitudes: bfloat16 [8, 1536, 1536], P('pair', 'grid'), may hold values from -6 to 6
- packed_factor: bfloat16 [512, 512], P(('grid', 'pair')), may hold values from -0.25 to 0.25
- screen: int32 [4, 4], replicated, may hold values from 0 to 11, as said below
- metric: bfloat16 [512, 512], P(None, 'grid'), may hold values from -6 to 6
- occ_energy: float32 [300], replicated, may hold values from -1.5 to -0.3
- vir_energy: float32 [1536], replicated, may hold values from 0.2 to 3
- pair_occ: int32 [8, 2], P('pair'), may hold values from 0 to 299
Outputs:
- update: float32 [8, 1536, 1536], P('pair', 'grid')
The draws below stay inside these ranges and needn't reach their ends.
Inputs may be any that keep to these rules, and one draw needn't show every extreme that they name: `screen`: each row lists 4 different virtual tiles.
All inputs are finite; a program needn't handle non-finite values.
Results may differ from the reference program's by a relative error of at most 0.0049.
Values may be sent and summed in bfloat16 or wider, within the bound.
No kernel may reach another device: no remote copies, remote signals or barrier semaphores. Data moves between devices by JAX's collectives and lax.ppermute only.
A program may use at most 64 MiB of HBM per device.

```python
import jax
import jax.numpy as jnp
from jax import lax

V = 1536
O = 300
TILE = 128
BLOCK = 128
S = 4
NP = 512
PAIRS = 8


def draw_screen(key, part):
    key = jax.random.fold_in(key, 7)
    number_of_tiles = V // TILE
    block_count = NP // BLOCK
    raw = jax.random.randint(key, (block_count, number_of_tiles), 0, 1 << 20)
    tile_list = jnp.arange(number_of_tiles, dtype=jnp.int32)[None, :]
    block_list = jnp.arange(block_count, dtype=jnp.int32)[:, None]
    screen_scores = raw * number_of_tiles + tile_list
    extra_credit = (block_list == 0) & (tile_list == number_of_tiles - 1) | (block_list == 1) & (tile_list == 0)
    screen_scores = screen_scores + jnp.where(extra_credit, (1 << 22) * number_of_tiles, 0)
    order = jnp.argsort(-screen_scores, axis=1, stable=True)
    return order[:, :S].astype(jnp.int32)


def plant(values, key, low, top_value):
    dims = values.shape
    spot = [jax.random.randint(jax.random.fold_in(key, axis), (), 0, dims[axis]) for axis in range(len(dims))]
    values = values.at[tuple(spot)].set(low)
    longest = dims.index(max(dims))
    spot[longest] = (spot[longest] + 1) % dims[longest]
    return values.at[tuple(spot)].set(top_value)


def level_of(key, dims, cuts, least, top_value):
    factor_of = 1.0
    for dim, blocks in cuts:
        steps = jax.random.uniform(jax.random.fold_in(jax.random.fold_in(key, 6), dim), (blocks,), jnp.float32, least / len(cuts), top_value / len(cuts))
        factor_of = factor_of * jnp.repeat(jnp.exp(steps), dims[dim] // blocks).reshape((-1,) + (1,) * (len(dims) - 1 - dim))
    return factor_of


def normal_values(stream_key, shape, deviation, most, cuts=(), kind=jnp.bfloat16):
    drawn = deviation * jax.random.normal(stream_key, shape, jnp.float32)
    if cuts:
        drawn = drawn * level_of(stream_key, shape, cuts, -0.22, 0.18)
    return jnp.clip(drawn, -most, most).astype(kind)


def setup_inputs(seed: int = 0) -> dict:
    streams_of = jax.random.split(jax.random.key(seed), 8)
    amplitudes = normal_values(streams_of[0], (PAIRS, V, V), 1.0, 6.0, ((0, 8), (1, 4)))
    packed_factor = normal_values(streams_of[1], (NP, S * TILE), (S * TILE) ** -0.5, 0.25, ((0, 32),))
    screen = draw_screen(jax.random.fold_in(streams_of[7], 71), 0)
    metric = normal_values(streams_of[3], (NP, NP), 1.0, 6.0, ((1, 4),))
    occ_energy = jnp.clip(jax.random.uniform(streams_of[4], (O,), jnp.float32, -1.5, -0.3), -1.5, -0.3)
    vir_energy = jnp.clip(jax.random.uniform(streams_of[5], (V,), jnp.float32, 0.2, 3.0), 0.2, 3.0)
    pair_occ = plant(jax.random.randint(streams_of[6], (PAIRS, 2), 0, O), jax.random.fold_in(streams_of[6], 1), 0, O - 1).astype(jnp.int32)
    return {"amplitudes": amplitudes, "packed_factor": packed_factor, "screen": screen, "metric": metric, "occ_energy": occ_energy, "vir_energy": vir_energy, "pair_occ": pair_occ}


def widened_factor(packed, screen, number_of_tiles):
    block_count, slots = screen.shape
    tile_rows = packed.shape[1] // slots
    block_rows = packed.shape[0] // block_count
    onehot = (screen[:, :, None] == jnp.arange(number_of_tiles, dtype=jnp.int32)[None, None, :]).astype(jnp.bfloat16)
    pieces = packed.reshape(block_count, block_rows, slots, tile_rows)
    dense_factor = jnp.einsum('bst,bpse->tebp', onehot.astype(jnp.float32), pieces.astype(jnp.float32))
    return dense_factor.reshape(number_of_tiles * tile_rows, block_count * block_rows).astype(jnp.bfloat16)


def reference(amplitudes, packed_factor, screen, metric, occ_energy, vir_energy, pair_occ):
    factor = widened_factor(packed_factor, screen, V // TILE)
    metric_wide = metric.astype(jnp.float32)

    def per_pair(inputs):
        single_amplitude, occ_pair = inputs
        half_product = jnp.dot(single_amplitude, factor, preferred_element_type=jnp.float32).astype(jnp.bfloat16)
        mixed = jnp.dot(factor.T, half_product, preferred_element_type=jnp.float32)
        weighted = (metric_wide * mixed).astype(jnp.bfloat16)
        ladder = jnp.dot(factor, weighted, preferred_element_type=jnp.float32).astype(jnp.bfloat16)
        result = jnp.dot(ladder, factor.T, preferred_element_type=jnp.float32)
        occ_total = occ_energy[occ_pair[0]] + occ_energy[occ_pair[1]]
        denominator = (vir_energy[:, None] + vir_energy[None, :]) - occ_total
        return result / denominator

    return lax.map(per_pair, (amplitudes, pair_occ))
```

```python
import functools

import jax
import jax.numpy as jnp
from jax import lax
from jax.experimental import pallas as pl
from jax.experimental.pallas import tpu as pltpu
from jax.sharding import PartitionSpec as P

BF16 = jnp.bfloat16
F32 = jnp.float32
VMEM_LIMIT = 40 * 1024 * 1024


def exchange(value, axis, size, step):
    return lax.ppermute(value, axis, [(i, i ^ step) for i in range(size)])


def pack_kernel(tile, slots, count, place, screen, amplitudes, *rest):
    outs, sems = rest[:count], rest[count]
    copies = []
    for k in list(range(1, count)) + [0]:
        block = place[0] ^ k
        for s in range(slots):
            column = pl.multiple_of(screen[block, s] * tile, tile)
            copies.append(
                pltpu.make_async_copy(
                    amplitudes.at[:, pl.ds(column, tile)],
                    outs[k].at[:, pl.ds(s * tile, tile)],
                    sems.at[k * slots + s],
                )
            )
    for copy in copies:
        copy.start()
    for copy in copies:
        copy.wait()


def pack(place, screen, amplitudes, count, tile):
    rows = amplitudes.shape[0]
    slots = screen.shape[1]
    return pl.pallas_call(
        functools.partial(pack_kernel, tile, slots, count),
        out_shape=[jax.ShapeDtypeStruct((rows, slots * tile), BF16)] * count,
        in_specs=[
            pl.BlockSpec(memory_space=pltpu.SMEM),
            pl.BlockSpec(memory_space=pltpu.SMEM),
            pl.BlockSpec(memory_space=pl.ANY),
        ],
        out_specs=[pl.BlockSpec(memory_space=pl.ANY)] * count,
        scratch_shapes=[pltpu.SemaphoreType.DMA((count * slots,))],
        name="pack",
    )(place, screen, amplitudes)


def widen_kernel(tile, slots, screen, packed, dense):
    width = packed.shape[0] // screen.shape[0]
    dense[...] = jnp.zeros_like(dense)
    for b in range(screen.shape[0]):
        for s in range(slots):
            column = pl.multiple_of(screen[b, s] * tile, tile)
            dense[b * width : (b + 1) * width, pl.ds(column, tile)] = packed[
                b * width : (b + 1) * width, s * tile : (s + 1) * tile
            ]


def widen(screen, packed, virtuals, tile):
    return pl.pallas_call(
        functools.partial(widen_kernel, tile, screen.shape[1]),
        out_shape=jax.ShapeDtypeStruct((packed.shape[0], virtuals), BF16),
        in_specs=[
            pl.BlockSpec(memory_space=pltpu.SMEM),
            pl.BlockSpec(memory_space=pltpu.VMEM),
        ],
        out_specs=pl.BlockSpec(memory_space=pltpu.VMEM),
        compiler_params=pltpu.CompilerParams(vmem_limit_bytes=VMEM_LIMIT),
        name="widen",
    )(screen, packed)


def ladder_kernel(tile, slots, count, place, screen, packed, metric, *rest):
    amps, outs = rest[:count], rest[count : 2 * count]
    half, selected, total = rest[2 * count :]
    width = metric.shape[1]
    rows = amps[0].shape[0]
    me = place[0]
    own = packed[pl.ds(pl.multiple_of(me * width, width), width), :]
    for k in range(count):
        start = pl.multiple_of((me ^ k) * rows, rows)
        half[pl.ds(start, rows), :] = lax.dot_general(
            amps[k][...], own, (((1,), (1,)), ((), ())), preferred_element_type=F32
        ).astype(BF16)
    total[...] = jnp.zeros_like(total)
    for b in range(count):
        for s in range(slots):
            start = pl.multiple_of(screen[b, s] * tile, tile)
            selected[b, s * tile : (s + 1) * tile, :] = half[pl.ds(start, tile), :]
    for b in range(count):
        block = packed[b * width : (b + 1) * width, :]
        mixed = jnp.dot(block, selected[b], preferred_element_type=F32)
        weighted = (metric[b * width : (b + 1) * width, :].astype(F32) * mixed).astype(BF16)
        part = lax.dot_general(
            block, weighted, (((0,), (0,)), ((), ())), preferred_element_type=F32
        )
        for s in range(slots):
            start = pl.multiple_of(screen[b, s] * tile, tile)
            total[pl.ds(start, tile), :] += part[s * tile : (s + 1) * tile, :]
    for k in range(count):
        start = pl.multiple_of((me ^ k) * rows, rows)
        outs[k][...] = total[pl.ds(start, rows), :].astype(BF16)


def ladders(place, screen, packed, metric, amps, virtuals, tile):
    count = len(amps)
    rows = amps[0].shape[0]
    width = metric.shape[1]
    slots = screen.shape[1]
    vmem = pl.BlockSpec(memory_space=pltpu.VMEM)
    return pl.pallas_call(
        functools.partial(ladder_kernel, tile, slots, count),
        out_shape=[jax.ShapeDtypeStruct((rows, width), BF16)] * count,
        in_specs=[pl.BlockSpec(memory_space=pltpu.SMEM)] * 2 + [vmem] * (2 + count),
        out_specs=[vmem] * count,
        scratch_shapes=[
            pltpu.VMEM((virtuals, width), BF16),
            pltpu.VMEM((count, slots * tile, width), BF16),
            pltpu.VMEM((virtuals, width), F32),
        ],
        compiler_params=pltpu.CompilerParams(vmem_limit_bytes=VMEM_LIMIT),
        name="ladders",
    )(place, screen, packed, metric, *amps)


def result_kernel(count, place, pair_occ, occ_energy, own_vir, vir, dense, *rest):
    pieces, out, joined = rest[:count], rest[count], rest[count + 1]
    me = place[0]
    width = pieces[0].shape[1]
    for k in range(count):
        column = pl.multiple_of((me ^ k) * width, width)
        joined[:, pl.ds(column, width)] = pieces[k][...]
    occ_total = occ_energy[pair_occ[0, 0]] + occ_energy[pair_occ[0, 1]]
    value = jnp.dot(joined[...], dense[...], preferred_element_type=F32)
    out[...] = value / ((own_vir[...] + vir[...]) - occ_total)


def results(place, pair_occ, occ_energy, own_vir, vir, dense, pieces):
    count = len(pieces)
    rows, width = pieces[0].shape
    points, virtuals = dense.shape
    steps = 3 if rows % 48 == 0 else 1
    part = rows // steps
    smem = pl.BlockSpec(memory_space=pltpu.SMEM)
    return pl.pallas_call(
        functools.partial(result_kernel, count),
        grid=(steps,),
        out_shape=jax.ShapeDtypeStruct((rows, virtuals), F32),
        in_specs=[smem] * 3
        + [
            pl.BlockSpec((part, 1), lambda i: (i, 0)),
            pl.BlockSpec((1, virtuals), lambda i: (0, 0)),
            pl.BlockSpec((points, virtuals), lambda i: (0, 0)),
        ]
        + [pl.BlockSpec((part, width), lambda i: (i, 0))] * count,
        out_specs=pl.BlockSpec((part, virtuals), lambda i: (i, 0)),
        scratch_shapes=[pltpu.VMEM((part, points), BF16)],
        compiler_params=pltpu.CompilerParams(vmem_limit_bytes=VMEM_LIMIT),
        name="results",
    )(place, pair_occ, occ_energy, own_vir, vir, dense, *pieces)


def local(
    grids, pairs, amplitudes, packed_factor, screen, metric, occ_energy, vir_energy, pair_occ
):
    me = lax.axis_index("grid")
    pair = lax.axis_index("pair")
    layer, core = pair // 2, pair % 2
    layers = pairs // 2
    place = me.astype(jnp.int32).reshape(1)
    _, rows, virtuals = amplitudes.shape
    tile = packed_factor.shape[1] // screen.shape[1]

    packs = pack(place, screen, amplitudes[0], grids, tile)
    amps = [packs[0]] + [exchange(packs[k], "grid", grids, k) for k in range(1, grids)]

    stack = jnp.zeros((layers,) + packed_factor.shape, BF16)
    stack = lax.dynamic_update_slice(stack, packed_factor[None], (layer, 0, 0))
    for k in range(1, layers):
        piece = exchange(packed_factor, "pair", pairs, 2 * k)
        stack = lax.dynamic_update_slice(stack, piece[None], (layer ^ k, 0, 0))
    plane = jnp.zeros((grids,) + stack.shape, BF16)
    plane = lax.dynamic_update_slice(plane, stack[None], (me, 0, 0, 0))
    for k in range(1, grids):
        piece = exchange(stack, "grid", grids, k)
        plane = lax.dynamic_update_slice(plane, piece[None], (me ^ k, 0, 0, 0))
    other = exchange(plane, "pair", pairs, 1)
    packed = jnp.where(
        core == 0, jnp.stack([plane, other], 2), jnp.stack([other, plane], 2)
    ).reshape(-1, packed_factor.shape[1])
    dense = widen(screen, packed, virtuals, tile)
    own_vir = lax.dynamic_slice_in_dim(vir_energy, me * rows, rows, 0)[:, None]

    sent = ladders(place, screen, packed, metric, amps, virtuals, tile)
    pieces = [sent[0]] + [exchange(sent[k], "grid", grids, k) for k in range(1, grids)]
    update = results(
        place, pair_occ, occ_energy, own_vir, vir_energy[None, :], dense, pieces
    )
    return update[None]


def solution(mesh):
    in_specs = (
        P("pair", "grid", None),
        P(("grid", "pair"), None),
        P(),
        P(None, "grid"),
        P(),
        P(),
        P("pair", None),
    )
    return jax.shard_map(
        functools.partial(local, mesh.shape["grid"], mesh.shape["pair"]),
        mesh=mesh,
        in_specs=in_specs,
        out_specs=P("pair", "grid", None),
        check_vma=False,
    )
```

```python
import functools

import jax
import jax.numpy as jnp
from jax import lax
from jax.experimental import pallas as pl
from jax.experimental.pallas import tpu as pltpu
from jax.sharding import PartitionSpec as P

BF16 = jnp.bfloat16
F32 = jnp.float32
VMEM_LIMIT = 40 * 1024 * 1024


def exchange(value, axis, size, step):
    return lax.ppermute(value, axis, [(i, i ^ step) for i in range(size)])


def pack_kernel(tile, slots, count, place, screen, amplitudes, *rest):
    outs, sems = rest[:count], rest[count]
    copies = []
    for k in list(range(1, count)) + [0]:
        block = place[0] ^ k
        for s in range(slots):
            column = pl.multiple_of(screen[block, s] * tile, tile)
            copies.append(
                pltpu.make_async_copy(
                    amplitudes.at[:, pl.ds(column, tile)],
                    outs[k].at[:, pl.ds(s * tile, tile)],
                    sems.at[k * slots + s],
                )
            )
    for copy in copies:
        copy.start()
    for copy in copies:
        copy.wait()


def pack(place, screen, amplitudes, count, tile):
    rows = amplitudes.shape[0]
    slots = screen.shape[1]
    return pl.pallas_call(
        functools.partial(pack_kernel, tile, slots, count),
        out_shape=[jax.ShapeDtypeStruct((rows, slots * tile), BF16)] * count,
        in_specs=[
            pl.BlockSpec(memory_space=pltpu.SMEM),
            pl.BlockSpec(memory_space=pltpu.SMEM),
            pl.BlockSpec(memory_space=pl.ANY),
        ],
        out_specs=[pl.BlockSpec(memory_space=pltpu.VMEM)] * count,
        scratch_shapes=[pltpu.SemaphoreType.DMA((count * slots,))],
        cost_estimate=pl.CostEstimate(
            flops=0, bytes_accessed=4 * count * rows * slots * tile, transcendentals=0
        ),
        compiler_params=pltpu.CompilerParams(vmem_limit_bytes=VMEM_LIMIT),
        name="pack",
    )(place, screen, amplitudes)


def half_kernel(listed, block, out):
    out[...] = lax.dot_general(
        listed[...], block[...], (((1,), (1,)), ((), ())), preferred_element_type=F32
    ).astype(BF16)


def half_product(listed, block):
    rows, columns = listed.shape
    width = block.shape[0]
    vmem = pl.BlockSpec(memory_space=pltpu.VMEM)
    return pl.pallas_call(
        half_kernel,
        out_shape=jax.ShapeDtypeStruct((rows, width), BF16),
        in_specs=[vmem] * 2,
        out_specs=vmem,
        cost_estimate=pl.CostEstimate(
            flops=2 * rows * columns * width, bytes_accessed=0, transcendentals=0
        ),
        compiler_params=pltpu.CompilerParams(vmem_limit_bytes=VMEM_LIMIT),
        name="half_product",
    )(listed, block)


def prepare_kernel(tile, slots, count, place, screen, pair_occ, occ_energy, own_vir, vir, *rest):
    blocks, (dense, turned, inverse) = rest[:count], rest[count:]
    width = blocks[0].shape[0]
    dense[...] = jnp.zeros_like(dense)
    for k in range(count):
        b = place[0] ^ k
        for s in range(slots):
            column = pl.multiple_of(screen[b, s] * tile, tile)
            dense[k * width : (k + 1) * width, pl.ds(column, tile)] = blocks[k][
                :, s * tile : (s + 1) * tile
            ]
        turned[k] = blocks[k][...].T
    occ_total = occ_energy[pair_occ[0, 0]] + occ_energy[pair_occ[0, 1]]
    inverse[...] = 1.0 / ((own_vir[...] + vir[...]) - occ_total)


def prepare(place, screen, pair_occ, occ_energy, own_vir, vir, blocks, tile):
    count = len(blocks)
    width, columns = blocks[0].shape
    rows, virtuals = own_vir.shape[0], vir.shape[1]
    smem = pl.BlockSpec(memory_space=pltpu.SMEM)
    vmem = pl.BlockSpec(memory_space=pltpu.VMEM)
    return pl.pallas_call(
        functools.partial(prepare_kernel, tile, screen.shape[1], count),
        out_shape=[
            jax.ShapeDtypeStruct((count * width, virtuals), BF16),
            jax.ShapeDtypeStruct((count, columns, width), BF16),
            jax.ShapeDtypeStruct((rows, virtuals), F32),
        ],
        in_specs=[smem] * 4 + [vmem] * (2 + count),
        out_specs=[vmem] * 3,
        compiler_params=pltpu.CompilerParams(vmem_limit_bytes=VMEM_LIMIT),
        name="prepare",
    )(place, screen, pair_occ, occ_energy, own_vir, vir, *blocks)


def ladder_kernel(tile, slots, count, place, screen, turned, metric, *rest):
    blocks, halves, outs = (rest[i * count : (i + 1) * count] for i in range(3))
    half, total = rest[3 * count :]
    width = metric.shape[1]
    rows = halves[0].shape[0]
    me = place[0]
    for k in range(count):
        start = pl.multiple_of((me ^ k) * rows, rows)
        half[pl.ds(start, rows), :] = halves[k][...]
    total[...] = jnp.zeros_like(total)
    for k in range(count):
        b = me ^ k
        starts = [pl.multiple_of(screen[b, s] * tile, tile) for s in range(slots)]
        listed = jnp.concatenate([half[pl.ds(start, tile), :] for start in starts], axis=0)
        mixed = jnp.dot(blocks[k][...], listed, preferred_element_type=F32)
        scale = metric[pl.ds(pl.multiple_of(b * width, width), width), :].astype(F32)
        weighted = (scale * mixed).astype(BF16)
        part = jnp.dot(turned[k], weighted, preferred_element_type=F32)
        for s, start in enumerate(starts):
            total[pl.ds(start, tile), :] += part[s * tile : (s + 1) * tile, :]
    for k in range(count):
        start = pl.multiple_of((me ^ k) * rows, rows)
        outs[k][...] = total[pl.ds(start, rows), :].astype(BF16)


def ladders(place, screen, turned, metric, blocks, halves, virtuals, tile):
    count = len(halves)
    rows, width = halves[0].shape
    slots = screen.shape[1]
    smem = pl.BlockSpec(memory_space=pltpu.SMEM)
    vmem = pl.BlockSpec(memory_space=pltpu.VMEM)
    return pl.pallas_call(
        functools.partial(ladder_kernel, tile, slots, count),
        out_shape=[jax.ShapeDtypeStruct((rows, width), BF16)] * count,
        in_specs=[smem] * 2 + [vmem] * (2 + 2 * count),
        out_specs=[vmem] * count,
        scratch_shapes=[pltpu.VMEM((virtuals, width), BF16), pltpu.VMEM((virtuals, width), F32)],
        compiler_params=pltpu.CompilerParams(vmem_limit_bytes=VMEM_LIMIT),
        name="ladders",
    )(place, screen, turned, metric, *blocks, *halves)


def result_kernel(count, chunks, dense, inverse, *rest):
    pieces, out = rest[:count], rest[count]
    joined, staged, sems = rest[count + 1 :]
    width = pieces[0].shape[1]
    part = out.shape[1] // chunks
    for k in range(count):
        joined[:, k * width : (k + 1) * width] = pieces[k][...]
    copies = []
    for j in range(chunks):
        span = slice(j * part, (j + 1) * part)
        value = jnp.dot(joined[...], dense[:, span], preferred_element_type=F32)
        staged[:, span] = value * inverse[:, span]
        copies.append(pltpu.make_async_copy(staged.at[:, span], out.at[:, span], sems.at[j]))
        copies[-1].start()
    for copy in copies:
        copy.wait()


def results(dense, inverse, pieces):
    count = len(pieces)
    rows = pieces[0].shape[0]
    points, virtuals = dense.shape
    chunks = 6 if virtuals % 768 == 0 else 1
    vmem = pl.BlockSpec(memory_space=pltpu.VMEM)
    return pl.pallas_call(
        functools.partial(result_kernel, count, chunks),
        out_shape=jax.ShapeDtypeStruct((rows, virtuals), F32),
        in_specs=[vmem] * (2 + count),
        out_specs=pl.BlockSpec(memory_space=pl.ANY),
        scratch_shapes=[
            pltpu.VMEM((rows, points), BF16),
            pltpu.VMEM((rows, virtuals), F32),
            pltpu.SemaphoreType.DMA((chunks,)),
        ],
        compiler_params=pltpu.CompilerParams(vmem_limit_bytes=VMEM_LIMIT),
        name="results",
    )(dense, inverse, *pieces)


def local(
    grids, pairs, amplitudes, packed_factor, screen, metric, occ_energy, vir_energy, pair_occ
):
    me = lax.axis_index("grid")
    pair = lax.axis_index("pair")
    place = me.astype(jnp.int32).reshape(1)
    _, rows, virtuals = amplitudes.shape
    tile = packed_factor.shape[1] // screen.shape[1]

    block = packed_factor[None]
    step = 2
    while step < pairs:
        other = exchange(block, "pair", pairs, step)
        block = jnp.where(
            pair & step == 0,
            jnp.concatenate([block, other], 0),
            jnp.concatenate([other, block], 0),
        )
        step *= 2
    other = exchange(block, "pair", pairs, 1)
    block = jnp.where(
        pair & 1 == 0, jnp.stack([block, other], 1), jnp.stack([other, block], 1)
    ).reshape(-1, packed_factor.shape[1])
    blocks = [block] + [exchange(block, "grid", grids, k) for k in range(1, grids)]

    packs = pack(place, screen, amplitudes[0], grids, tile)
    halves = [half_product(packs[0], block)]
    for k in range(1, grids):
        half = half_product(packs[k], blocks[k])
        if k + 1 < grids:
            half, blocks[k + 1] = lax.optimization_barrier((half, blocks[k + 1]))
        halves.append(exchange(half, "grid", grids, k))

    own_vir = lax.dynamic_slice_in_dim(vir_energy, me * rows, rows, 0)[:, None]
    dense, turned, inverse = prepare(
        place, screen, pair_occ, occ_energy, own_vir, vir_energy[None, :], blocks, tile
    )
    sent = ladders(place, screen, turned, metric, blocks, halves, virtuals, tile)
    pieces = [sent[0]] + [exchange(sent[k], "grid", grids, k) for k in range(1, grids)]
    return results(dense, inverse, pieces)[None]


def solution(mesh):
    in_specs = (
        P("pair", "grid", None),
        P(("grid", "pair"), None),
        P(),
        P(None, "grid"),
        P(),
        P(),
        P("pair", None),
    )
    return jax.shard_map(
        functools.partial(local, mesh.shape["grid"], mesh.shape["pair"]),
        mesh=mesh,
        in_specs=in_specs,
        out_specs=P("pair", "grid", None),
        check_vma=False,
    )
```

```python
import functools

import jax
import jax.numpy as jnp
from jax import lax
from jax.experimental import pallas as pl
from jax.experimental.pallas import tpu as pltpu
from jax.sharding import PartitionSpec as P

BF16 = jnp.bfloat16
F32 = jnp.float32
VMEM_LIMIT = 40 * 1024 * 1024


def exchange(value, axis, size, step):
    return lax.ppermute(value, axis, [(i, i ^ step) for i in range(size)])


def keep_kernel(value, out):
    out[...] = value[...]


def keep(value):
    vmem = pl.BlockSpec(memory_space=pltpu.VMEM)
    return pl.pallas_call(
        keep_kernel,
        out_shape=pltpu.VMEM(value.shape, value.dtype),
        in_specs=[vmem],
        out_specs=vmem,
        name="keep",
    )(value)


def pack_kernel(tile, slots, count, place, screen, amplitudes, *rest):
    outs, sems = rest[:count], rest[count]
    copies = []
    for k in range(count):
        block = place[0] ^ k
        for s in range(slots):
            column = pl.multiple_of(screen[block, s] * tile, tile)
            copies.append(
                pltpu.make_async_copy(
                    amplitudes.at[:, pl.ds(column, tile)],
                    outs[k].at[:, pl.ds(s * tile, tile)],
                    sems.at[k * slots + s],
                )
            )
    for copy in copies:
        copy.start()
    for copy in copies:
        copy.wait()


def pack(place, screen, amplitudes, tile):
    rows = amplitudes.shape[0]
    count, slots = screen.shape
    smem = pl.BlockSpec(memory_space=pltpu.SMEM)
    hbm = pl.BlockSpec(memory_space=pltpu.HBM)
    return pl.pallas_call(
        functools.partial(pack_kernel, tile, slots, count),
        out_shape=[jax.ShapeDtypeStruct((rows, slots * tile), BF16)] * count,
        in_specs=[smem] * 2 + [hbm],
        out_specs=[pl.BlockSpec(memory_space=pltpu.VMEM)] * count,
        scratch_shapes=[pltpu.SemaphoreType.DMA((count * slots,))],
        cost_estimate=pl.CostEstimate(
            flops=0, bytes_accessed=4 * count * rows * slots * tile, transcendentals=0
        ),
        compiler_params=pltpu.CompilerParams(vmem_limit_bytes=VMEM_LIMIT),
        name="pack",
    )(place, screen, amplitudes)


def half_kernel(count, packed, *rest):
    listed, outs = rest[:count], rest[count:]
    width = packed.shape[0] // count
    for k in range(count):
        outs[k][...] = lax.dot_general(
            listed[k][...],
            packed[k * width : (k + 1) * width, :],
            (((1,), (1,)), ((), ())),
            preferred_element_type=F32,
        ).astype(BF16)


def half_products(packed, listed):
    count = len(listed)
    rows, columns = listed[0].shape
    width = packed.shape[0] // count
    vmem = pl.BlockSpec(memory_space=pltpu.VMEM)
    return pl.pallas_call(
        functools.partial(half_kernel, count),
        out_shape=[jax.ShapeDtypeStruct((rows, width), BF16)] * count,
        in_specs=[vmem] * (1 + count),
        out_specs=[vmem] * count,
        compiler_params=pltpu.CompilerParams(vmem_limit_bytes=VMEM_LIMIT),
        name="half_products",
    )(packed, *listed)


def prepare_kernel(tile, slots, count, place, screen, pair_occ, occ_energy, *rest):
    packed, metric, own_vir, vir, dense, turned, scale, inverse = rest
    width = packed.shape[0] // count
    dense[...] = jnp.zeros_like(dense)
    turned[...] = jnp.zeros_like(turned)
    for k in range(count):
        b = place[0] ^ k
        span = slice(k * width, (k + 1) * width)
        block = packed[span, :]
        other = block.T
        for s in range(slots):
            start = pl.multiple_of(screen[b, s] * tile, tile)
            dense[span, pl.ds(start, tile)] = block[:, s * tile : (s + 1) * tile]
            turned[pl.ds(start, tile), span] = other[s * tile : (s + 1) * tile, :]
        scale[:, span] = metric[pl.ds(pl.multiple_of(b * width, width), width), :].astype(F32).T
    occ_total = occ_energy[pair_occ[0, 0]] + occ_energy[pair_occ[0, 1]]
    inverse[...] = 1.0 / ((own_vir[...] + vir[...]) - occ_total)


def prepare(place, screen, pair_occ, occ_energy, packed, metric, own_vir, vir, tile):
    count, slots = screen.shape
    points = packed.shape[0]
    rows, virtuals = own_vir.shape[0], vir.shape[1]
    smem = pl.BlockSpec(memory_space=pltpu.SMEM)
    vmem = pl.BlockSpec(memory_space=pltpu.VMEM)
    return pl.pallas_call(
        functools.partial(prepare_kernel, tile, slots, count),
        out_shape=[
            jax.ShapeDtypeStruct((points, virtuals), BF16),
            jax.ShapeDtypeStruct((virtuals, points), BF16),
            jax.ShapeDtypeStruct((metric.shape[1], points), F32),
            jax.ShapeDtypeStruct((rows, virtuals), F32),
        ],
        in_specs=[smem] * 4 + [vmem] * 4,
        out_specs=[vmem] * 4,
        cost_estimate=pl.CostEstimate(
            flops=0, bytes_accessed=8 * points * virtuals, transcendentals=0
        ),
        compiler_params=pltpu.CompilerParams(vmem_limit_bytes=VMEM_LIMIT),
        name="prepare",
    )(place, screen, pair_occ, occ_energy, packed, metric, own_vir, vir)


def mixed_part(half, factor):
    return lax.dot_general(half, factor, (((0,), (0,)), ((), ())), preferred_element_type=F32)


def mixed_kernel(known, place, turned, *rest):
    halves, out = rest[:known], rest[known]
    rows = halves[0].shape[0]
    total = None
    for k in range(known):
        start = pl.multiple_of((place[0] ^ k) * rows, rows)
        part = mixed_part(halves[k][...], turned[pl.ds(start, rows), :])
        total = part if total is None else total + part
    out[...] = total


def mixed_sum(place, turned, halves):
    known = len(halves)
    width, points = halves[0].shape[1], turned.shape[1]
    vmem = pl.BlockSpec(memory_space=pltpu.VMEM)
    return pl.pallas_call(
        functools.partial(mixed_kernel, known),
        out_shape=jax.ShapeDtypeStruct((width, points), F32),
        in_specs=[pl.BlockSpec(memory_space=pltpu.SMEM)] + [vmem] * (1 + known),
        out_specs=vmem,
        cost_estimate=pl.CostEstimate(
            flops=2 * known * halves[0].size * points, bytes_accessed=0, transcendentals=0
        ),
        compiler_params=pltpu.CompilerParams(vmem_limit_bytes=VMEM_LIMIT),
        name="mixed",
    )(place, turned, *halves)


def ladder_kernel(count, turned, scale, mixed, half, *outs):
    me = lax.axis_index("grid")
    rows = half.shape[0]
    start = pl.multiple_of((me ^ (count - 1)) * rows, rows)
    total = mixed[...] + mixed_part(half[...], turned[pl.ds(start, rows), :])
    weighted = (scale[...] * total).astype(BF16)
    for k in list(range(1, count)) + [0]:
        start = pl.multiple_of((me ^ k) * rows, rows)
        outs[k][...] = lax.dot_general(
            turned[pl.ds(start, rows), :],
            weighted,
            (((1,), (1,)), ((), ())),
            preferred_element_type=F32,
        ).astype(BF16)


def ladders(turned, scale, mixed, half, count):
    rows, width = half.shape
    vmem = pl.BlockSpec(memory_space=pltpu.VMEM)
    return pl.pallas_call(
        functools.partial(ladder_kernel, count),
        out_shape=[jax.ShapeDtypeStruct((rows, width), BF16)] * count,
        in_specs=[vmem] * 4,
        out_specs=[vmem] * count,
        compiler_params=pltpu.CompilerParams(vmem_limit_bytes=VMEM_LIMIT),
        name="ladders",
    )(turned, scale, mixed, half)


def start_kernel(dense, *rest):
    pieces, out = rest[:-1], rest[-1]
    joined = jnp.concatenate([piece[...] for piece in pieces], axis=1)
    out[...] = jnp.dot(joined, dense[: joined.shape[1], :], preferred_element_type=F32)


def result_start(dense, pieces):
    rows, width = pieces[0].shape
    vmem = pl.BlockSpec(memory_space=pltpu.VMEM)
    return pl.pallas_call(
        start_kernel,
        out_shape=jax.ShapeDtypeStruct((rows, dense.shape[1]), F32),
        in_specs=[vmem] * (1 + len(pieces)),
        out_specs=vmem,
        cost_estimate=pl.CostEstimate(
            flops=2 * len(pieces) * rows * width * dense.shape[1],
            bytes_accessed=0,
            transcendentals=0,
        ),
        compiler_params=pltpu.CompilerParams(vmem_limit_bytes=VMEM_LIMIT),
        name="result_start",
    )(dense, *pieces)


def result_kernel(chunks, begun, dense, inverse, *rest):
    *pieces, out, staged, sems = rest
    joined = jnp.concatenate([piece[...] for piece in pieces], axis=1)
    first = dense.shape[0] - joined.shape[1]
    part = out.shape[1] // chunks
    copies = []
    for j in range(chunks):
        span = slice(j * part, (j + 1) * part)
        value = jnp.dot(joined, dense[first:, span], preferred_element_type=F32)
        staged[:, span] = (begun[:, span] + value) * inverse[:, span]
        copies.append(pltpu.make_async_copy(staged.at[:, span], out.at[:, span], sems.at[j]))
        copies[-1].start()
    for copy in copies:
        copy.wait()


def results(begun, dense, inverse, pieces):
    rows, virtuals = begun.shape
    chunks = 6 if virtuals % 768 == 0 else 1
    vmem = pl.BlockSpec(memory_space=pltpu.VMEM)
    return pl.pallas_call(
        functools.partial(result_kernel, chunks),
        out_shape=jax.ShapeDtypeStruct((rows, virtuals), F32),
        in_specs=[vmem] * (3 + len(pieces)),
        out_specs=pl.BlockSpec(memory_space=pl.ANY),
        scratch_shapes=[
            pltpu.VMEM((rows, virtuals), F32),
            pltpu.SemaphoreType.DMA((chunks,)),
        ],
        compiler_params=pltpu.CompilerParams(vmem_limit_bytes=VMEM_LIMIT),
        name="results",
    )(begun, dense, inverse, *pieces)


def local(
    grids, pairs, amplitudes, packed_factor, screen, metric, occ_energy, vir_energy, pair_occ
):
    me = lax.axis_index("grid")
    pair = lax.axis_index("pair")
    place = me.astype(jnp.int32).reshape(1)
    rows = amplitudes.shape[1]
    tile = packed_factor.shape[1] // screen.shape[1]

    part, sent = keep(packed_factor)[None], packed_factor[None]
    step = 2
    while step < pairs:
        other = exchange(sent, "pair", pairs, step)
        part = jnp.where(
            pair & step == 0,
            jnp.concatenate([part, other], 0),
            jnp.concatenate([other, part], 0),
        )
        sent = part
        step *= 2
    amplitudes, part = lax.optimization_barrier((amplitudes, part))
    packs = pack(place, screen, amplitudes[0], tile)
    part = jnp.stack([part] + [exchange(part, "grid", grids, k) for k in range(1, grids)], 0)
    packs, part = lax.optimization_barrier((packs, part))
    other = exchange(part, "pair", pairs, 1)
    packed = jnp.where(
        pair & 1 == 0, jnp.stack([part, other], 2), jnp.stack([other, part], 2)
    ).reshape(-1, packed_factor.shape[1])

    own_vir = lax.dynamic_slice_in_dim(vir_energy, me * rows, rows, 0)[:, None]
    halves = half_products(packed, packs)
    halves = [halves[0]] + [exchange(halves[k], "grid", grids, k) for k in range(1, grids)]
    dense, turned, scale, inverse = prepare(
        place, screen, pair_occ, occ_energy, packed, metric, own_vir, vir_energy[None, :], tile
    )
    mixed = mixed_sum(place, turned, halves[:-1])
    sent = ladders(turned, scale, mixed, halves[-1], grids)
    pieces = [sent[0]] + [exchange(sent[k], "grid", grids, k) for k in range(1, grids)]
    begun = result_start(dense, pieces[: grids // 2])
    return results(begun, dense, inverse, pieces[grids // 2 :])[None]


def solution(mesh):
    in_specs = (
        P("pair", "grid", None),
        P(("grid", "pair"), None),
        P(),
        P(None, "grid"),
        P(),
        P(),
        P("pair", None),
    )
    return jax.shard_map(
        functools.partial(local, mesh.shape["grid"], mesh.shape["pair"]),
        mesh=mesh,
        in_specs=in_specs,
        out_specs=P("pair", "grid", None),
        check_vma=False,
    )
```

```python
import functools

import jax
import jax.numpy as jnp
from jax import lax
from jax.experimental import pallas as pl
from jax.experimental.pallas import tpu as pltpu
from jax.sharding import PartitionSpec as P

BF16 = jnp.bfloat16
F32 = jnp.float32
VMEM_LIMIT = 40 * 1024 * 1024


def exchange(value, axis, size, step):
    return lax.ppermute(value, axis, [(i, i ^ step) for i in range(size)])


def keep_kernel(value, out):
    out[...] = value[...]


def keep(value):
    vmem = pl.BlockSpec(memory_space=pltpu.VMEM)
    return pl.pallas_call(
        keep_kernel,
        out_shape=pltpu.VMEM(value.shape, value.dtype),
        in_specs=[vmem],
        out_specs=vmem,
        name="keep",
    )(value)


def pack_kernel(tile, slots, count, place, screen, amplitudes, *rest):
    outs, sems = rest[:count], rest[count]
    copies = []
    for k in range(count):
        block = place[0] ^ k
        for s in range(slots):
            column = pl.multiple_of(screen[block, s] * tile, tile)
            copies.append(
                pltpu.make_async_copy(
                    amplitudes.at[:, pl.ds(column, tile)],
                    outs[k].at[:, pl.ds(s * tile, tile)],
                    sems.at[k * slots + s],
                )
            )
    for copy in copies:
        copy.start()
    for copy in copies:
        copy.wait()


def pack(place, screen, amplitudes, tile):
    rows = amplitudes.shape[0]
    count, slots = screen.shape
    smem = pl.BlockSpec(memory_space=pltpu.SMEM)
    hbm = pl.BlockSpec(memory_space=pltpu.HBM)
    return pl.pallas_call(
        functools.partial(pack_kernel, tile, slots, count),
        out_shape=[jax.ShapeDtypeStruct((rows, slots * tile), BF16)] * count,
        in_specs=[smem] * 2 + [hbm],
        out_specs=[pl.BlockSpec(memory_space=pltpu.VMEM)] * count,
        scratch_shapes=[pltpu.SemaphoreType.DMA((count * slots,))],
        cost_estimate=pl.CostEstimate(
            flops=0, bytes_accessed=4 * count * rows * slots * tile, transcendentals=0
        ),
        compiler_params=pltpu.CompilerParams(vmem_limit_bytes=VMEM_LIMIT),
        name="pack",
    )(place, screen, amplitudes)


def half_kernel(count, *refs):
    for k in range(count):
        refs[2 * count + k][...] = lax.dot_general(
            refs[k][...],
            refs[count + k][...],
            (((1,), (1,)), ((), ())),
            preferred_element_type=F32,
        ).astype(BF16)


def half_products(listed, blocks):
    count = len(listed)
    rows, columns = listed[0].shape
    width = blocks[0].shape[0]
    vmem = pl.BlockSpec(memory_space=pltpu.VMEM)
    return pl.pallas_call(
        functools.partial(half_kernel, count),
        out_shape=[jax.ShapeDtypeStruct((rows, width), BF16)] * count,
        in_specs=[vmem] * (2 * count),
        out_specs=[vmem] * count,
        cost_estimate=pl.CostEstimate(
            flops=2 * count * rows * columns * width, bytes_accessed=0, transcendentals=0
        ),
        compiler_params=pltpu.CompilerParams(vmem_limit_bytes=VMEM_LIMIT),
        name="half_products",
    )(*listed, *blocks)


def prepare_kernel(tile, slots, count, place, screen, pair_occ, occ_energy, *rest):
    blocks = rest[:count]
    metric, own_vir, vir, dense, turned, scale, inverse = rest[count:]
    width = blocks[0].shape[0]
    dense[...] = jnp.zeros_like(dense)
    turned[...] = jnp.zeros_like(turned)
    for k in range(count):
        b = place[0] ^ k
        span = slice(k * width, (k + 1) * width)
        block = blocks[k][...]
        other = block.T
        for s in range(slots):
            start = pl.multiple_of(screen[b, s] * tile, tile)
            dense[span, pl.ds(start, tile)] = block[:, s * tile : (s + 1) * tile]
            turned[pl.ds(start, tile), span] = other[s * tile : (s + 1) * tile, :]
        scale[:, span] = metric[pl.ds(pl.multiple_of(b * width, width), width), :].astype(F32).T
    occ_total = occ_energy[pair_occ[0, 0]] + occ_energy[pair_occ[0, 1]]
    inverse[...] = 1.0 / ((own_vir[...] + vir[...]) - occ_total)


def prepare(place, screen, pair_occ, occ_energy, blocks, metric, own_vir, vir, tile):
    count, slots = screen.shape
    points = count * blocks[0].shape[0]
    rows, virtuals = own_vir.shape[0], vir.shape[1]
    smem = pl.BlockSpec(memory_space=pltpu.SMEM)
    vmem = pl.BlockSpec(memory_space=pltpu.VMEM)
    return pl.pallas_call(
        functools.partial(prepare_kernel, tile, slots, count),
        out_shape=[
            jax.ShapeDtypeStruct((points, virtuals), BF16),
            jax.ShapeDtypeStruct((virtuals, points), BF16),
            jax.ShapeDtypeStruct((metric.shape[1], points), F32),
            jax.ShapeDtypeStruct((rows, virtuals), F32),
        ],
        in_specs=[smem] * 4 + [vmem] * (3 + count),
        out_specs=[vmem] * 4,
        cost_estimate=pl.CostEstimate(
            flops=0, bytes_accessed=8 * points * virtuals, transcendentals=0
        ),
        compiler_params=pltpu.CompilerParams(vmem_limit_bytes=VMEM_LIMIT),
        name="prepare",
    )(place, screen, pair_occ, occ_energy, *blocks, metric, own_vir, vir)


def mixed_part(half, factor):
    return lax.dot_general(half, factor, (((0,), (0,)), ((), ())), preferred_element_type=F32)


def mixed_kernel(order, place, turned, *rest):
    halves, out = rest[:-1], rest[-1]
    rows = halves[0].shape[0]
    total = None
    for k, half in zip(order, halves):
        start = pl.multiple_of((place[0] ^ k) * rows, rows)
        part = mixed_part(half[...], turned[pl.ds(start, rows), :])
        total = part if total is None else total + part
    out[...] = total


def mixed_sum(order, place, turned, halves):
    known = len(halves)
    width, points = halves[0].shape[1], turned.shape[1]
    vmem = pl.BlockSpec(memory_space=pltpu.VMEM)
    return pl.pallas_call(
        functools.partial(mixed_kernel, order),
        out_shape=jax.ShapeDtypeStruct((width, points), F32),
        in_specs=[pl.BlockSpec(memory_space=pltpu.SMEM)] + [vmem] * (1 + known),
        out_specs=vmem,
        cost_estimate=pl.CostEstimate(
            flops=2 * known * halves[0].size * points, bytes_accessed=0, transcendentals=0
        ),
        compiler_params=pltpu.CompilerParams(vmem_limit_bytes=VMEM_LIMIT),
        name="mixed",
    )(place, turned, *halves)


def ladder_kernel(order, late, turned, scale, mixed, *rest):
    halves, outs = rest[: len(late)], rest[len(late) :]
    me = lax.axis_index("grid")
    rows = halves[0].shape[0]

    def own_rows(k):
        return turned[pl.ds(pl.multiple_of((me ^ k) * rows, rows), rows), :]

    total = mixed[...]
    for k, half in zip(late, halves):
        total = total + mixed_part(half[...], own_rows(k))
    weighted = (scale[...] * total).astype(BF16)
    for k in order:
        outs[k][...] = lax.dot_general(
            own_rows(k), weighted, (((1,), (1,)), ((), ())), preferred_element_type=F32
        ).astype(BF16)


def ladders(order, late, turned, scale, mixed, halves):
    rows, width = halves[0].shape
    vmem = pl.BlockSpec(memory_space=pltpu.VMEM)
    return pl.pallas_call(
        functools.partial(ladder_kernel, order, late),
        out_shape=[jax.ShapeDtypeStruct((rows, width), BF16)] * len(order),
        in_specs=[vmem] * (3 + len(halves)),
        out_specs=[vmem] * len(order),
        compiler_params=pltpu.CompilerParams(vmem_limit_bytes=VMEM_LIMIT),
        name="ladders",
    )(turned, scale, mixed, *halves)


def joined(order, width, pieces, dense, span):
    total = None
    for k, piece in zip(order, pieces):
        block = dense[k * width : (k + 1) * width, span]
        part = jnp.dot(piece[...], block, preferred_element_type=F32)
        total = part if total is None else total + part
    return total


def start_kernel(order, dense, *rest):
    pieces, out = rest[:-1], rest[-1]
    out[...] = joined(order, pieces[0].shape[1], pieces, dense, slice(None))


def result_start(order, dense, pieces):
    rows, width = pieces[0].shape
    vmem = pl.BlockSpec(memory_space=pltpu.VMEM)
    return pl.pallas_call(
        functools.partial(start_kernel, order),
        out_shape=jax.ShapeDtypeStruct((rows, dense.shape[1]), F32),
        in_specs=[vmem] * (1 + len(pieces)),
        out_specs=vmem,
        cost_estimate=pl.CostEstimate(
            flops=2 * len(pieces) * rows * width * dense.shape[1],
            bytes_accessed=0,
            transcendentals=0,
        ),
        compiler_params=pltpu.CompilerParams(vmem_limit_bytes=VMEM_LIMIT),
        name="result_start",
    )(dense, *pieces)


def result_kernel(order, chunks, begun, dense, inverse, *rest):
    *pieces, out, staged, sems = rest
    width = pieces[0].shape[1]
    part = out.shape[1] // chunks
    copies = []
    for j in range(chunks):
        span = slice(j * part, (j + 1) * part)
        value = joined(order, width, pieces, dense, span)
        staged[:, span] = (begun[:, span] + value) * inverse[:, span]
        copies.append(pltpu.make_async_copy(staged.at[:, span], out.at[:, span], sems.at[j]))
        copies[-1].start()
    for copy in copies:
        copy.wait()


def results(order, begun, dense, inverse, pieces):
    rows, virtuals = begun.shape
    chunks = 6 if virtuals % 768 == 0 else 1
    vmem = pl.BlockSpec(memory_space=pltpu.VMEM)
    return pl.pallas_call(
        functools.partial(result_kernel, order, chunks),
        out_shape=jax.ShapeDtypeStruct((rows, virtuals), F32),
        in_specs=[vmem] * (3 + len(pieces)),
        out_specs=pl.BlockSpec(memory_space=pl.ANY),
        scratch_shapes=[
            pltpu.VMEM((rows, virtuals), F32),
            pltpu.SemaphoreType.DMA((chunks,)),
        ],
        compiler_params=pltpu.CompilerParams(vmem_limit_bytes=VMEM_LIMIT),
        name="results",
    )(begun, dense, inverse, *pieces)


def local(
    grids, pairs, amplitudes, packed_factor, screen, metric, occ_energy, vir_energy, pair_occ
):
    me = lax.axis_index("grid")
    pair = lax.axis_index("pair")
    place = me.astype(jnp.int32).reshape(1)
    order = [0] + list(range(grids - 1, 0, -1))
    rows = amplitudes.shape[1]
    tile = packed_factor.shape[1] // screen.shape[1]

    part, sent = keep(packed_factor)[None], packed_factor[None]
    step = 2
    while step < pairs:
        other = exchange(sent, "pair", pairs, step)
        part = jnp.where(
            pair & step == 0,
            jnp.concatenate([part, other], 0),
            jnp.concatenate([other, part], 0),
        )
        sent = part
        step *= 2
        amplitudes, part = lax.optimization_barrier((amplitudes, part))
    parts = [exchange(part, "grid", grids, k) if k else part for k in range(grids)]
    packs = pack(place, screen, amplitudes[0], tile)
    packs = list(packs)
    blocks = []
    for k, part in enumerate(parts):
        part, packs[k] = lax.optimization_barrier((part, packs[k]))
        other = exchange(part, "pair", pairs, 1)
        both = jnp.where(
            pair & 1 == 0, jnp.stack([part, other], 1), jnp.stack([other, part], 1)
        )
        blocks.append(both.reshape(-1, packed_factor.shape[1]))

    halves = []
    for ks in ([0], order[1:2], order[2:]):
        group = half_products([packs[k] for k in ks], [blocks[k] for k in ks])
        halves += [exchange(half, "grid", grids, k) if k else half for k, half in zip(ks, group)]
    vir_energy, halves[0] = lax.optimization_barrier((vir_energy, halves[0]))
    own_vir = lax.dynamic_slice_in_dim(vir_energy, me * rows, rows, 0)[:, None]
    dense, turned, scale, inverse = prepare(
        place, screen, pair_occ, occ_energy, blocks, metric, own_vir, vir_energy[None, :], tile
    )
    early = grids // 2
    mixed = mixed_sum(order[:early], place, turned, halves[:early])
    sent = ladders(order, order[early:], turned, scale, mixed, halves[early:])
    pieces = [exchange(sent[k], "grid", grids, k) if k else sent[k] for k in order]
    begun = result_start(order[:early], dense, pieces[:early])
    return results(order[early:], begun, dense, inverse, pieces[early:])[None]


def solution(mesh):
    in_specs = (
        P("pair", "grid", None),
        P(("grid", "pair"), None),
        P(),
        P(None, "grid"),
        P(),
        P(),
        P("pair", None),
    )
    return jax.shard_map(
        functools.partial(local, mesh.shape["grid"], mesh.shape["pair"]),
        mesh=mesh,
        in_specs=in_specs,
        out_specs=P("pair", "grid", None),
        check_vma=False,
    )
```

```python
import functools

import jax
import jax.numpy as jnp
from jax import lax
from jax.experimental import pallas as pl
from jax.experimental.pallas import tpu as pltpu
from jax.sharding import PartitionSpec as P

BF16 = jnp.bfloat16
F32 = jnp.float32
VMEM_LIMIT = 40 * 1024 * 1024


def exchange(value, axis, size, step):
    return lax.ppermute(value, axis, [(i, i ^ step) for i in range(size)])


def keep_kernel(value, out):
    out[...] = value[...]


def keep(value):
    vmem = pl.BlockSpec(memory_space=pltpu.VMEM)
    return pl.pallas_call(
        keep_kernel,
        out_shape=pltpu.VMEM(value.shape, value.dtype),
        in_specs=[vmem],
        out_specs=vmem,
        name="keep",
    )(value)


def pack_kernel(tile, slots, count, place, screen, amplitudes, *rest):
    outs, sems = rest[:count], rest[count]
    copies = []
    for k in range(count):
        block = place[0] ^ k
        for s in range(slots):
            column = pl.multiple_of(screen[block, s] * tile, tile)
            copies.append(
                pltpu.make_async_copy(
                    amplitudes.at[:, pl.ds(column, tile)],
                    outs[k].at[:, pl.ds(s * tile, tile)],
                    sems.at[k * slots + s],
                )
            )
    for copy in copies:
        copy.start()
    for copy in copies:
        copy.wait()


def pack(place, screen, amplitudes, tile):
    rows = amplitudes.shape[0]
    count, slots = screen.shape
    smem = pl.BlockSpec(memory_space=pltpu.SMEM)
    hbm = pl.BlockSpec(memory_space=pltpu.HBM)
    return pl.pallas_call(
        functools.partial(pack_kernel, tile, slots, count),
        out_shape=[jax.ShapeDtypeStruct((rows, slots * tile), BF16)] * count,
        in_specs=[smem] * 2 + [hbm],
        out_specs=[pl.BlockSpec(memory_space=pltpu.VMEM)] * count,
        scratch_shapes=[pltpu.SemaphoreType.DMA((count * slots,))],
        cost_estimate=pl.CostEstimate(
            flops=0, bytes_accessed=4 * count * rows * slots * tile, transcendentals=0
        ),
        compiler_params=pltpu.CompilerParams(vmem_limit_bytes=VMEM_LIMIT),
        name="pack",
    )(place, screen, amplitudes)


def half_kernel(count, *refs):
    for k in range(count):
        refs[2 * count + k][...] = lax.dot_general(
            refs[k][...],
            refs[count + k][...],
            (((1,), (1,)), ((), ())),
            preferred_element_type=F32,
        ).astype(BF16)


def half_products(listed, blocks):
    count = len(listed)
    rows, columns = listed[0].shape
    width = blocks[0].shape[0]
    vmem = pl.BlockSpec(memory_space=pltpu.VMEM)
    return pl.pallas_call(
        functools.partial(half_kernel, count),
        out_shape=[jax.ShapeDtypeStruct((rows, width), BF16)] * count,
        in_specs=[vmem] * (2 * count),
        out_specs=[vmem] * count,
        cost_estimate=pl.CostEstimate(
            flops=2 * count * rows * columns * width, bytes_accessed=0, transcendentals=0
        ),
        compiler_params=pltpu.CompilerParams(vmem_limit_bytes=VMEM_LIMIT),
        name="half_products",
    )(*listed, *blocks)


def prepare_kernel(tile, slots, count, place, screen, pair_occ, occ_energy, *rest):
    blocks = rest[:count]
    metric, own_vir, vir, dense, turned, scale, inverse = rest[count:]
    width = blocks[0].shape[0]
    dense[...] = jnp.zeros_like(dense)
    turned[...] = jnp.zeros_like(turned)
    for k in range(count):
        b = place[0] ^ k
        span = slice(k * width, (k + 1) * width)
        block = blocks[k][...]
        other = block.T
        for s in range(slots):
            start = pl.multiple_of(screen[b, s] * tile, tile)
            dense[span, pl.ds(start, tile)] = block[:, s * tile : (s + 1) * tile]
            turned[pl.ds(start, tile), span] = other[s * tile : (s + 1) * tile, :]
        scale[:, span] = metric[pl.ds(pl.multiple_of(b * width, width), width), :].astype(F32).T
    occ_total = occ_energy[pair_occ[0, 0]] + occ_energy[pair_occ[0, 1]]
    inverse[...] = 1.0 / ((own_vir[...] + vir[...]) - occ_total)


def prepare(place, screen, pair_occ, occ_energy, blocks, metric, own_vir, vir, tile):
    count, slots = screen.shape
    points = count * blocks[0].shape[0]
    rows, virtuals = own_vir.shape[0], vir.shape[1]
    smem = pl.BlockSpec(memory_space=pltpu.SMEM)
    vmem = pl.BlockSpec(memory_space=pltpu.VMEM)
    return pl.pallas_call(
        functools.partial(prepare_kernel, tile, slots, count),
        out_shape=[
            jax.ShapeDtypeStruct((points, virtuals), BF16),
            jax.ShapeDtypeStruct((virtuals, points), BF16),
            jax.ShapeDtypeStruct((metric.shape[1], points), F32),
            jax.ShapeDtypeStruct((rows, virtuals), F32),
        ],
        in_specs=[smem] * 4 + [vmem] * (3 + count),
        out_specs=[vmem] * 4,
        cost_estimate=pl.CostEstimate(
            flops=0, bytes_accessed=8 * points * virtuals, transcendentals=0
        ),
        compiler_params=pltpu.CompilerParams(vmem_limit_bytes=VMEM_LIMIT),
        name="prepare",
    )(place, screen, pair_occ, occ_energy, *blocks, metric, own_vir, vir)


def mixed_part(half, factor):
    return lax.dot_general(half, factor, (((0,), (0,)), ((), ())), preferred_element_type=F32)


def mixed_kernel(order, place, turned, *rest):
    halves, out = rest[:-1], rest[-1]
    rows = halves[0].shape[0]
    total = None
    for k, half in zip(order, halves):
        start = pl.multiple_of((place[0] ^ k) * rows, rows)
        part = mixed_part(half[...], turned[pl.ds(start, rows), :])
        total = part if total is None else total + part
    out[...] = total


def mixed_sum(order, place, turned, halves):
    known = len(halves)
    width, points = halves[0].shape[1], turned.shape[1]
    vmem = pl.BlockSpec(memory_space=pltpu.VMEM)
    return pl.pallas_call(
        functools.partial(mixed_kernel, order),
        out_shape=jax.ShapeDtypeStruct((width, points), F32),
        in_specs=[pl.BlockSpec(memory_space=pltpu.SMEM)] + [vmem] * (1 + known),
        out_specs=vmem,
        cost_estimate=pl.CostEstimate(
            flops=2 * known * halves[0].size * points, bytes_accessed=0, transcendentals=0
        ),
        compiler_params=pltpu.CompilerParams(vmem_limit_bytes=VMEM_LIMIT),
        name="mixed",
    )(place, turned, *halves)


def ladder_kernel(order, late, turned, scale, mixed, *rest):
    halves, outs = rest[: len(late)], rest[len(late) :]
    me = lax.axis_index("grid")
    rows = halves[0].shape[0]

    def own_rows(k):
        return turned[pl.ds(pl.multiple_of((me ^ k) * rows, rows), rows), :]

    total = mixed[...]
    for k, half in zip(late, halves):
        total = total + mixed_part(half[...], own_rows(k))
    weighted = (scale[...] * total).astype(BF16)
    for k in order:
        outs[k][...] = lax.dot_general(
            own_rows(k), weighted, (((1,), (1,)), ((), ())), preferred_element_type=F32
        ).astype(BF16)


def ladders(order, late, turned, scale, mixed, halves):
    rows, width = halves[0].shape
    vmem = pl.BlockSpec(memory_space=pltpu.VMEM)
    return pl.pallas_call(
        functools.partial(ladder_kernel, order, late),
        out_shape=[jax.ShapeDtypeStruct((rows, width), BF16)] * len(order),
        in_specs=[vmem] * (3 + len(halves)),
        out_specs=[vmem] * len(order),
        compiler_params=pltpu.CompilerParams(vmem_limit_bytes=VMEM_LIMIT),
        name="ladders",
    )(turned, scale, mixed, *halves)


def joined(order, width, pieces, dense, span):
    total = None
    for k, piece in zip(order, pieces):
        block = dense[k * width : (k + 1) * width, span]
        part = jnp.dot(piece[...], block, preferred_element_type=F32)
        total = part if total is None else total + part
    return total


def start_kernel(order, dense, *rest):
    pieces, out = rest[:-1], rest[-1]
    out[...] = joined(order, pieces[0].shape[1], pieces, dense, slice(None))


def result_start(order, dense, pieces):
    rows, width = pieces[0].shape
    vmem = pl.BlockSpec(memory_space=pltpu.VMEM)
    return pl.pallas_call(
        functools.partial(start_kernel, order),
        out_shape=jax.ShapeDtypeStruct((rows, dense.shape[1]), F32),
        in_specs=[vmem] * (1 + len(pieces)),
        out_specs=vmem,
        cost_estimate=pl.CostEstimate(
            flops=2 * len(pieces) * rows * width * dense.shape[1],
            bytes_accessed=0,
            transcendentals=0,
        ),
        compiler_params=pltpu.CompilerParams(vmem_limit_bytes=VMEM_LIMIT),
        name="result_start",
    )(dense, *pieces)


def result_kernel(order, chunks, begun, dense, inverse, *rest):
    *pieces, out, staged, sems = rest
    width = pieces[0].shape[1]
    part = out.shape[1] // chunks
    copies = []
    for j in range(chunks):
        span = slice(j * part, (j + 1) * part)
        value = joined(order, width, pieces, dense, span)
        staged[:, span] = (begun[:, span] + value) * inverse[:, span]
        copies.append(pltpu.make_async_copy(staged.at[:, span], out.at[:, span], sems.at[j]))
        copies[-1].start()
    for copy in copies:
        copy.wait()


def results(order, begun, dense, inverse, pieces):
    rows, virtuals = begun.shape
    chunks = 6 if virtuals % 768 == 0 else 1
    vmem = pl.BlockSpec(memory_space=pltpu.VMEM)
    return pl.pallas_call(
        functools.partial(result_kernel, order, chunks),
        out_shape=jax.ShapeDtypeStruct((rows, virtuals), F32),
        in_specs=[vmem] * (3 + len(pieces)),
        out_specs=pl.BlockSpec(memory_space=pl.ANY),
        scratch_shapes=[
            pltpu.VMEM((rows, virtuals), F32),
            pltpu.SemaphoreType.DMA((chunks,)),
        ],
        compiler_params=pltpu.CompilerParams(vmem_limit_bytes=VMEM_LIMIT),
        name="results",
    )(begun, dense, inverse, *pieces)


def local(
    grids, pairs, amplitudes, packed_factor, screen, metric, occ_energy, vir_energy, pair_occ
):
    me = lax.axis_index("grid")
    pair = lax.axis_index("pair")
    place = me.astype(jnp.int32).reshape(1)
    order = [0] + list(range(grids - 1, 0, -1))
    rows = amplitudes.shape[1]
    tile = packed_factor.shape[1] // screen.shape[1]

    part, sent = keep(packed_factor)[None], packed_factor[None]
    step = 2
    while step < pairs:
        other = exchange(sent, "pair", pairs, step)
        part = jnp.where(
            pair & step == 0,
            jnp.concatenate([part, other], 0),
            jnp.concatenate([other, part], 0),
        )
        sent = part
        step *= 2
        ready, part = lax.optimization_barrier((place, part))
    parts = [exchange(part, "grid", grids, k) if k else part for k in range(grids)]
    packs = pack(ready, screen, amplitudes[0], tile)
    def swapped(part):
        other = exchange(part, "pair", pairs, 1)
        both = jnp.where(
            pair & 1 == 0, jnp.stack([part, other], 1), jnp.stack([other, part], 1)
        )
        return both.reshape(-1, packed_factor.shape[1])

    packs = list(packs)
    blocks = [None] * grids
    for k in order[1:]:
        part, packs[k] = lax.optimization_barrier((parts[k], packs[k]))
        blocks[k] = swapped(part)
    halves = []
    for ks in (order[1:2], order[2:]):
        group = half_products([packs[k] for k in ks], [blocks[k] for k in ks])
        if not halves:
            parts[0], group = lax.optimization_barrier((parts[0], group))
        halves += [exchange(half, "grid", grids, k) for k, half in zip(ks, group)]
    blocks[0] = swapped(parts[0])
    halves = list(half_products([packs[0]], [blocks[0]])) + halves
    vir_energy, halves[0] = lax.optimization_barrier((vir_energy, halves[0]))
    own_vir = lax.dynamic_slice_in_dim(vir_energy, me * rows, rows, 0)[:, None]
    dense, turned, scale, inverse = prepare(
        place, screen, pair_occ, occ_energy, blocks, metric, own_vir, vir_energy[None, :], tile
    )
    early = grids // 2
    mixed = mixed_sum(order[:early], place, turned, halves[:early])
    sent = ladders(order, order[early:], turned, scale, mixed, halves[early:])
    pieces = [exchange(sent[k], "grid", grids, k) if k else sent[k] for k in order]
    begun = result_start(order[:early], dense, pieces[:early])
    return results(order[early:], begun, dense, inverse, pieces[early:])[None]


def solution(mesh):
    in_specs = (
        P("pair", "grid", None),
        P(("grid", "pair"), None),
        P(),
        P(None, "grid"),
        P(),
        P(),
        P("pair", None),
    )
    return jax.shard_map(
        functools.partial(local, mesh.shape["grid"], mesh.shape["pair"]),
        mesh=mesh,
        in_specs=in_specs,
        out_specs=P("pair", "grid", None),
        check_vma=False,
    )
```

```python
import functools

import jax
import jax.numpy as jnp
from jax import lax
from jax.experimental import pallas as pl
from jax.experimental.pallas import tpu as pltpu
from jax.sharding import PartitionSpec as P

BF16 = jnp.bfloat16
F32 = jnp.float32
VMEM_LIMIT = 40 * 1024 * 1024


def exchange(value, axis, size, step):
    return lax.ppermute(value, axis, [(i, i ^ step) for i in range(size)])


def keep_kernel(value, out):
    out[...] = value[...]


def keep(value):
    vmem = pl.BlockSpec(memory_space=pltpu.VMEM)
    return pl.pallas_call(
        keep_kernel,
        out_shape=pltpu.VMEM(value.shape, value.dtype),
        in_specs=[vmem],
        out_specs=vmem,
        name="keep",
    )(value)


def pack_kernel(tile, slots, count, place, screen, amplitudes, *rest):
    outs, sems = rest[:count], rest[count]
    copies = []
    for k in range(count):
        block = place[0] ^ k
        for s in range(slots):
            column = pl.multiple_of(screen[block, s] * tile, tile)
            copies.append(
                pltpu.make_async_copy(
                    amplitudes.at[:, pl.ds(column, tile)],
                    outs[k].at[:, pl.ds(s * tile, tile)],
                    sems.at[k * slots + s],
                )
            )
    for copy in copies:
        copy.start()
    for copy in copies:
        copy.wait()


def pack(place, screen, amplitudes, tile):
    rows = amplitudes.shape[0]
    count, slots = screen.shape
    smem = pl.BlockSpec(memory_space=pltpu.SMEM)
    hbm = pl.BlockSpec(memory_space=pltpu.HBM)
    return pl.pallas_call(
        functools.partial(pack_kernel, tile, slots, count),
        out_shape=[jax.ShapeDtypeStruct((rows, slots * tile), BF16)] * count,
        in_specs=[smem] * 2 + [hbm],
        out_specs=[pl.BlockSpec(memory_space=pltpu.VMEM)] * count,
        scratch_shapes=[pltpu.SemaphoreType.DMA((count * slots,))],
        cost_estimate=pl.CostEstimate(
            flops=0, bytes_accessed=4 * count * rows * slots * tile, transcendentals=0
        ),
        compiler_params=pltpu.CompilerParams(vmem_limit_bytes=VMEM_LIMIT),
        name="pack",
    )(place, screen, amplitudes)


def half_kernel(count, *refs):
    for k in range(count):
        refs[2 * count + k][...] = lax.dot_general(
            refs[k][...],
            refs[count + k][...],
            (((1,), (1,)), ((), ())),
            preferred_element_type=F32,
        ).astype(BF16)


def half_products(listed, blocks):
    count = len(listed)
    rows, columns = listed[0].shape
    width = blocks[0].shape[0]
    vmem = pl.BlockSpec(memory_space=pltpu.VMEM)
    return pl.pallas_call(
        functools.partial(half_kernel, count),
        out_shape=[jax.ShapeDtypeStruct((rows, width), BF16)] * count,
        in_specs=[vmem] * (2 * count),
        out_specs=[vmem] * count,
        cost_estimate=pl.CostEstimate(
            flops=2 * count * rows * columns * width, bytes_accessed=0, transcendentals=0
        ),
        compiler_params=pltpu.CompilerParams(vmem_limit_bytes=VMEM_LIMIT),
        name="half_products",
    )(*listed, *blocks)


def prepare_kernel(tile, slots, count, place, screen, pair_occ, occ_energy, *rest):
    blocks = rest[:count]
    metric, own_vir, vir, dense, turned, scale, inverse = rest[count:]
    width = blocks[0].shape[0]
    dense[...] = jnp.zeros_like(dense)
    turned[...] = jnp.zeros_like(turned)
    for k in range(count):
        b = place[0] ^ k
        span = slice(k * width, (k + 1) * width)
        block = blocks[k][...]
        other = block.T
        for s in range(slots):
            start = pl.multiple_of(screen[b, s] * tile, tile)
            dense[span, pl.ds(start, tile)] = block[:, s * tile : (s + 1) * tile]
            turned[pl.ds(start, tile), span] = other[s * tile : (s + 1) * tile, :]
        scale[:, span] = metric[pl.ds(pl.multiple_of(b * width, width), width), :].astype(F32).T
    occ_total = occ_energy[pair_occ[0, 0]] + occ_energy[pair_occ[0, 1]]
    inverse[...] = 1.0 / ((own_vir[...] + vir[...]) - occ_total)


def prepare(place, screen, pair_occ, occ_energy, blocks, metric, own_vir, vir, tile):
    count, slots = screen.shape
    points = count * blocks[0].shape[0]
    rows, virtuals = own_vir.shape[0], vir.shape[1]
    smem = pl.BlockSpec(memory_space=pltpu.SMEM)
    vmem = pl.BlockSpec(memory_space=pltpu.VMEM)
    return pl.pallas_call(
        functools.partial(prepare_kernel, tile, slots, count),
        out_shape=[
            jax.ShapeDtypeStruct((points, virtuals), BF16),
            jax.ShapeDtypeStruct((virtuals, points), BF16),
            jax.ShapeDtypeStruct((metric.shape[1], points), F32),
            jax.ShapeDtypeStruct((rows, virtuals), F32),
        ],
        in_specs=[smem] * 4 + [vmem] * (3 + count),
        out_specs=[vmem] * 4,
        cost_estimate=pl.CostEstimate(
            flops=0, bytes_accessed=8 * points * virtuals, transcendentals=0
        ),
        compiler_params=pltpu.CompilerParams(vmem_limit_bytes=VMEM_LIMIT),
        name="prepare",
    )(place, screen, pair_occ, occ_energy, *blocks, metric, own_vir, vir)


def mixed_part(half, factor):
    return lax.dot_general(half, factor, (((0,), (0,)), ((), ())), preferred_element_type=F32)


def mixed_kernel(order, place, turned, *rest):
    halves, out = rest[:-1], rest[-1]
    rows = halves[0].shape[0]
    total = None
    for k, half in zip(order, halves):
        start = pl.multiple_of((place[0] ^ k) * rows, rows)
        part = mixed_part(half[...], turned[pl.ds(start, rows), :])
        total = part if total is None else total + part
    out[...] = total


def mixed_sum(order, place, turned, halves):
    known = len(halves)
    width, points = halves[0].shape[1], turned.shape[1]
    vmem = pl.BlockSpec(memory_space=pltpu.VMEM)
    return pl.pallas_call(
        functools.partial(mixed_kernel, order),
        out_shape=jax.ShapeDtypeStruct((width, points), F32),
        in_specs=[pl.BlockSpec(memory_space=pltpu.SMEM)] + [vmem] * (1 + known),
        out_specs=vmem,
        cost_estimate=pl.CostEstimate(
            flops=2 * known * halves[0].size * points, bytes_accessed=0, transcendentals=0
        ),
        compiler_params=pltpu.CompilerParams(vmem_limit_bytes=VMEM_LIMIT),
        name="mixed",
    )(place, turned, *halves)


def own_rows(turned, k, rows):
    start = (lax.axis_index("grid") ^ k) * rows
    return turned[pl.ds(pl.multiple_of(start, rows), rows), :]


def ladder_piece(turned, k, weighted, rows):
    return lax.dot_general(
        own_rows(turned, k, rows), weighted, (((1,), (1,)), ((), ())), preferred_element_type=F32
    ).astype(BF16)


def weighted_kernel(first, late, turned, scale, mixed, *rest):
    halves, (weighted, out) = rest[: len(late)], rest[len(late) :]
    rows = halves[0].shape[0]
    total = mixed[...]
    for k, half in zip(late, halves):
        total = total + mixed_part(half[...], own_rows(turned, k, rows))
    weighted[...] = (scale[...] * total).astype(BF16)
    out[...] = ladder_piece(turned, first, weighted[...], rows)


def ladder_kernel(ks, turned, weighted, *outs):
    for k, out in zip(ks, outs):
        out[...] = ladder_piece(turned, k, weighted[...], out.shape[0])


def ladders(order, late, turned, scale, mixed, halves):
    rows, width = halves[0].shape
    vmem = pl.BlockSpec(memory_space=pltpu.VMEM)
    piece = jax.ShapeDtypeStruct((rows, width), BF16)
    limit = pltpu.CompilerParams(vmem_limit_bytes=VMEM_LIMIT)
    pieces = {}
    weighted, pieces[order[1]] = pl.pallas_call(
        functools.partial(weighted_kernel, order[1], late),
        out_shape=[jax.ShapeDtypeStruct(scale.shape, BF16), piece],
        in_specs=[vmem] * (3 + len(halves)),
        out_specs=[vmem] * 2,
        compiler_params=limit,
        name="weighted",
    )(turned, scale, mixed, *halves)
    for ks in (order[2:], order[:1]):
        outs = pl.pallas_call(
            functools.partial(ladder_kernel, ks),
            out_shape=[piece] * len(ks),
            in_specs=[vmem] * 2,
            out_specs=[vmem] * len(ks),
            cost_estimate=pl.CostEstimate(
                flops=2 * len(ks) * rows * weighted.size, bytes_accessed=0, transcendentals=0
            ),
            compiler_params=limit,
            name="ladders",
        )(turned, weighted)
        pieces.update(zip(ks, outs))
    return [pieces[k] for k in range(len(order))]


def joined(order, width, pieces, dense, span):
    total = None
    for k, piece in zip(order, pieces):
        block = dense[k * width : (k + 1) * width, span]
        part = jnp.dot(piece[...], block, preferred_element_type=F32)
        total = part if total is None else total + part
    return total


def start_kernel(order, dense, *rest):
    pieces, out = rest[:-1], rest[-1]
    out[...] = joined(order, pieces[0].shape[1], pieces, dense, slice(None))


def result_start(order, dense, pieces):
    rows, width = pieces[0].shape
    vmem = pl.BlockSpec(memory_space=pltpu.VMEM)
    return pl.pallas_call(
        functools.partial(start_kernel, order),
        out_shape=jax.ShapeDtypeStruct((rows, dense.shape[1]), F32),
        in_specs=[vmem] * (1 + len(pieces)),
        out_specs=vmem,
        cost_estimate=pl.CostEstimate(
            flops=2 * len(pieces) * rows * width * dense.shape[1],
            bytes_accessed=0,
            transcendentals=0,
        ),
        compiler_params=pltpu.CompilerParams(vmem_limit_bytes=VMEM_LIMIT),
        name="result_start",
    )(dense, *pieces)


def result_kernel(order, chunks, begun, dense, inverse, *rest):
    *pieces, out, staged, sems = rest
    width = pieces[0].shape[1]
    part = out.shape[1] // chunks
    copies = []
    for j in range(chunks):
        span = slice(j * part, (j + 1) * part)
        value = joined(order, width, pieces, dense, span)
        staged[:, span] = (begun[:, span] + value) * inverse[:, span]
        copies.append(pltpu.make_async_copy(staged.at[:, span], out.at[:, span], sems.at[j]))
        copies[-1].start()
    for copy in copies:
        copy.wait()


def results(order, begun, dense, inverse, pieces):
    rows, virtuals = begun.shape
    chunks = 6 if virtuals % 768 == 0 else 1
    vmem = pl.BlockSpec(memory_space=pltpu.VMEM)
    return pl.pallas_call(
        functools.partial(result_kernel, order, chunks),
        out_shape=jax.ShapeDtypeStruct((rows, virtuals), F32),
        in_specs=[vmem] * (3 + len(pieces)),
        out_specs=pl.BlockSpec(memory_space=pl.ANY),
        scratch_shapes=[
            pltpu.VMEM((rows, virtuals), F32),
            pltpu.SemaphoreType.DMA((chunks,)),
        ],
        compiler_params=pltpu.CompilerParams(vmem_limit_bytes=VMEM_LIMIT),
        name="results",
    )(begun, dense, inverse, *pieces)


def local(
    grids, pairs, amplitudes, packed_factor, screen, metric, occ_energy, vir_energy, pair_occ
):
    me = lax.axis_index("grid")
    pair = lax.axis_index("pair")
    place = me.astype(jnp.int32).reshape(1)
    order = [0] + list(range(grids - 1, 0, -1))
    rows = amplitudes.shape[1]
    tile = packed_factor.shape[1] // screen.shape[1]

    part, sent = keep(packed_factor)[None], packed_factor[None]
    step = 2
    while step < pairs:
        other = exchange(sent, "pair", pairs, step)
        part = jnp.where(
            pair & step == 0,
            jnp.concatenate([part, other], 0),
            jnp.concatenate([other, part], 0),
        )
        sent = part
        step *= 2
        ready, part = lax.optimization_barrier((place, part))
    parts = [exchange(part, "grid", grids, k) if k else part for k in range(grids)]
    packs = pack(ready, screen, amplitudes[0], tile)
    def swapped(part):
        other = exchange(part, "pair", pairs, 1)
        both = jnp.where(
            pair & 1 == 0, jnp.stack([part, other], 1), jnp.stack([other, part], 1)
        )
        return both.reshape(-1, packed_factor.shape[1])

    packs = list(packs)
    blocks = [None] * grids
    for k in order[1:]:
        part, packs[k] = lax.optimization_barrier((parts[k], packs[k]))
        blocks[k] = swapped(part)
    halves = []
    for ks in (order[1:2], order[2:]):
        group = half_products([packs[k] for k in ks], [blocks[k] for k in ks])
        if not halves:
            parts[0], group = lax.optimization_barrier((parts[0], group))
        halves += [exchange(half, "grid", grids, k) for k, half in zip(ks, group)]
    blocks[0] = swapped(parts[0])
    halves = list(half_products([packs[0]], [blocks[0]])) + halves
    vir_energy, halves[0] = lax.optimization_barrier((vir_energy, halves[0]))
    own_vir = lax.dynamic_slice_in_dim(vir_energy, me * rows, rows, 0)[:, None]
    dense, turned, scale, inverse = prepare(
        place, screen, pair_occ, occ_energy, blocks, metric, own_vir, vir_energy[None, :], tile
    )
    early = grids // 2
    mixed = mixed_sum(order[:early], place, turned, halves[:early])
    sent = ladders(order, order[early:], turned, scale, mixed, halves[early:])
    pieces = [exchange(sent[k], "grid", grids, k) if k else sent[k] for k in order]
    begun = result_start(order[:early], dense, pieces[:early])
    return results(order[early:], begun, dense, inverse, pieces[early:])[None]


def solution(mesh):
    in_specs = (
        P("pair", "grid", None),
        P(("grid", "pair"), None),
        P(),
        P(None, "grid"),
        P(),
        P(),
        P("pair", None),
    )
    return jax.shard_map(
        functools.partial(local, mesh.shape["grid"], mesh.shape["pair"]),
        mesh=mesh,
        in_specs=in_specs,
        out_specs=P("pair", "grid", None),
        check_vma=False,
    )
```

```python
import functools

import jax
import jax.numpy as jnp
from jax import lax
from jax.experimental import pallas as pl
from jax.experimental.pallas import tpu as pltpu
from jax.sharding import PartitionSpec as P

BF16 = jnp.bfloat16
F32 = jnp.float32
VMEM_LIMIT = 40 * 1024 * 1024


def exchange(value, axis, size, step):
    return lax.ppermute(value, axis, [(i, i ^ step) for i in range(size)])


def keep_kernel(value, out):
    out[...] = value[...]


def keep(value):
    vmem = pl.BlockSpec(memory_space=pltpu.VMEM)
    return pl.pallas_call(
        keep_kernel,
        out_shape=pltpu.VMEM(value.shape, value.dtype),
        in_specs=[vmem],
        out_specs=vmem,
        name="keep",
    )(value)


def pack_kernel(tile, slots, count, place, screen, amplitudes, *rest):
    outs, sems = rest[:count], rest[count]
    copies = []
    for k in range(count):
        block = place[0] ^ k
        for s in range(slots):
            column = pl.multiple_of(screen[block, s] * tile, tile)
            copies.append(
                pltpu.make_async_copy(
                    amplitudes.at[:, pl.ds(column, tile)],
                    outs[k].at[:, pl.ds(s * tile, tile)],
                    sems.at[k * slots + s],
                )
            )
    for copy in copies:
        copy.start()
    for copy in copies:
        copy.wait()


def pack(place, screen, amplitudes, tile):
    rows = amplitudes.shape[0]
    count, slots = screen.shape
    smem = pl.BlockSpec(memory_space=pltpu.SMEM)
    hbm = pl.BlockSpec(memory_space=pltpu.HBM)
    return pl.pallas_call(
        functools.partial(pack_kernel, tile, slots, count),
        out_shape=[jax.ShapeDtypeStruct((rows, slots * tile), BF16)] * count,
        in_specs=[smem] * 2 + [hbm],
        out_specs=[pl.BlockSpec(memory_space=pltpu.VMEM)] * count,
        scratch_shapes=[pltpu.SemaphoreType.DMA((count * slots,))],
        cost_estimate=pl.CostEstimate(
            flops=0, bytes_accessed=4 * count * rows * slots * tile, transcendentals=0
        ),
        compiler_params=pltpu.CompilerParams(vmem_limit_bytes=VMEM_LIMIT),
        name="pack",
    )(place, screen, amplitudes)


def half_kernel(count, *refs):
    for k in range(count):
        refs[2 * count + k][...] = lax.dot_general(
            refs[k][...],
            refs[count + k][...],
            (((1,), (1,)), ((), ())),
            preferred_element_type=F32,
        ).astype(BF16)


def half_products(listed, blocks):
    count = len(listed)
    rows, columns = listed[0].shape
    width = blocks[0].shape[0]
    vmem = pl.BlockSpec(memory_space=pltpu.VMEM)
    return pl.pallas_call(
        functools.partial(half_kernel, count),
        out_shape=[jax.ShapeDtypeStruct((rows, width), BF16)] * count,
        in_specs=[vmem] * (2 * count),
        out_specs=[vmem] * count,
        cost_estimate=pl.CostEstimate(
            flops=2 * count * rows * columns * width, bytes_accessed=0, transcendentals=0
        ),
        compiler_params=pltpu.CompilerParams(vmem_limit_bytes=VMEM_LIMIT),
        name="half_products",
    )(*listed, *blocks)


def prepare_kernel(tile, slots, count, place, screen, pair_occ, occ_energy, *rest):
    blocks = rest[:count]
    metric, own_vir, vir, dense, turned, scale, inverse = rest[count:]
    width = blocks[0].shape[0]
    dense[...] = jnp.zeros_like(dense)
    turned[...] = jnp.zeros_like(turned)
    for k in range(count):
        b = place[0] ^ k
        span = slice(k * width, (k + 1) * width)
        block = blocks[k][...]
        other = block.T
        for s in range(slots):
            start = pl.multiple_of(screen[b, s] * tile, tile)
            dense[span, pl.ds(start, tile)] = block[:, s * tile : (s + 1) * tile]
            turned[pl.ds(start, tile), span] = other[s * tile : (s + 1) * tile, :]
        scale[:, span] = metric[pl.ds(pl.multiple_of(b * width, width), width), :].astype(F32).T
    occ_total = occ_energy[pair_occ[0, 0]] + occ_energy[pair_occ[0, 1]]
    inverse[...] = 1.0 / ((own_vir[...] + vir[...]) - occ_total)


def prepare(place, screen, pair_occ, occ_energy, blocks, metric, own_vir, vir, tile):
    count, slots = screen.shape
    points = count * blocks[0].shape[0]
    rows, virtuals = own_vir.shape[0], vir.shape[1]
    smem = pl.BlockSpec(memory_space=pltpu.SMEM)
    vmem = pl.BlockSpec(memory_space=pltpu.VMEM)
    return pl.pallas_call(
        functools.partial(prepare_kernel, tile, slots, count),
        out_shape=[
            jax.ShapeDtypeStruct((points, virtuals), BF16),
            jax.ShapeDtypeStruct((virtuals, points), BF16),
            jax.ShapeDtypeStruct((metric.shape[1], points), F32),
            jax.ShapeDtypeStruct((rows, virtuals), F32),
        ],
        in_specs=[smem] * 4 + [vmem] * (3 + count),
        out_specs=[vmem] * 4,
        cost_estimate=pl.CostEstimate(
            flops=0, bytes_accessed=8 * points * virtuals, transcendentals=0
        ),
        compiler_params=pltpu.CompilerParams(vmem_limit_bytes=VMEM_LIMIT),
        name="prepare",
    )(place, screen, pair_occ, occ_energy, *blocks, metric, own_vir, vir)


def mixed_part(half, factor):
    return lax.dot_general(half, factor, (((0,), (0,)), ((), ())), preferred_element_type=F32)


def mixed_kernel(order, place, turned, *rest):
    halves, out = rest[:-1], rest[-1]
    rows = halves[0].shape[0]
    total = None
    for k, half in zip(order, halves):
        start = pl.multiple_of((place[0] ^ k) * rows, rows)
        part = mixed_part(half[...], turned[pl.ds(start, rows), :])
        total = part if total is None else total + part
    out[...] = total


def mixed_sum(order, place, turned, halves):
    known = len(halves)
    width, points = halves[0].shape[1], turned.shape[1]
    vmem = pl.BlockSpec(memory_space=pltpu.VMEM)
    return pl.pallas_call(
        functools.partial(mixed_kernel, order),
        out_shape=jax.ShapeDtypeStruct((width, points), F32),
        in_specs=[pl.BlockSpec(memory_space=pltpu.SMEM)] + [vmem] * (1 + known),
        out_specs=vmem,
        cost_estimate=pl.CostEstimate(
            flops=2 * known * halves[0].size * points, bytes_accessed=0, transcendentals=0
        ),
        compiler_params=pltpu.CompilerParams(vmem_limit_bytes=VMEM_LIMIT),
        name="mixed",
    )(place, turned, *halves)


def own_rows(turned, k, rows):
    start = (lax.axis_index("grid") ^ k) * rows
    return turned[pl.ds(pl.multiple_of(start, rows), rows), :]


def ladder_piece(turned, k, weighted, rows):
    return lax.dot_general(
        own_rows(turned, k, rows), weighted, (((1,), (1,)), ((), ())), preferred_element_type=F32
    ).astype(BF16)


def weighted_kernel(first, late, turned, scale, mixed, *rest):
    halves, (weighted, out) = rest[: len(late)], rest[len(late) :]
    rows = halves[0].shape[0]
    total = mixed[...]
    for k, half in zip(late, halves):
        total = total + mixed_part(half[...], own_rows(turned, k, rows))
    weighted[...] = (scale[...] * total).astype(BF16)
    out[...] = ladder_piece(turned, first, weighted[...], rows)


def ladder_kernel(ks, turned, weighted, *outs):
    for k, out in zip(ks, outs):
        out[...] = ladder_piece(turned, k, weighted[...], out.shape[0])


def ladders(order, late, turned, scale, mixed, halves):
    rows, width = halves[0].shape
    vmem = pl.BlockSpec(memory_space=pltpu.VMEM)
    piece = jax.ShapeDtypeStruct((rows, width), BF16)
    limit = pltpu.CompilerParams(vmem_limit_bytes=VMEM_LIMIT)
    pieces = {}
    weighted, pieces[order[1]] = pl.pallas_call(
        functools.partial(weighted_kernel, order[1], late),
        out_shape=[jax.ShapeDtypeStruct(scale.shape, BF16), piece],
        in_specs=[vmem] * (3 + len(halves)),
        out_specs=[vmem] * 2,
        compiler_params=limit,
        name="weighted",
    )(turned, scale, mixed, *halves)
    for ks in (order[2:], order[:1]):
        outs = pl.pallas_call(
            functools.partial(ladder_kernel, ks),
            out_shape=[piece] * len(ks),
            in_specs=[vmem] * 2,
            out_specs=[vmem] * len(ks),
            cost_estimate=pl.CostEstimate(
                flops=2 * len(ks) * rows * weighted.size, bytes_accessed=0, transcendentals=0
            ),
            compiler_params=limit,
            name="ladders",
        )(turned, weighted)
        pieces.update(zip(ks, outs))
    return [pieces[k] for k in range(len(order))]


def joined(order, width, pieces, dense, span):
    total = None
    for k, piece in zip(order, pieces):
        block = dense[k * width : (k + 1) * width, span]
        part = jnp.dot(piece[...], block, preferred_element_type=F32)
        total = part if total is None else total + part
    return total


def start_kernel(order, dense, *rest):
    pieces, out = rest[:-1], rest[-1]
    out[...] = joined(order, pieces[0].shape[1], pieces, dense, slice(None))


def result_start(order, dense, pieces):
    rows, width = pieces[0].shape
    vmem = pl.BlockSpec(memory_space=pltpu.VMEM)
    return pl.pallas_call(
        functools.partial(start_kernel, order),
        out_shape=jax.ShapeDtypeStruct((rows, dense.shape[1]), F32),
        in_specs=[vmem] * (1 + len(pieces)),
        out_specs=vmem,
        cost_estimate=pl.CostEstimate(
            flops=2 * len(pieces) * rows * width * dense.shape[1],
            bytes_accessed=0,
            transcendentals=0,
        ),
        compiler_params=pltpu.CompilerParams(vmem_limit_bytes=VMEM_LIMIT),
        name="result_start",
    )(dense, *pieces)


def result_kernel(order, chunks, begun, dense, inverse, *rest):
    *pieces, out, staged, sems = rest
    width = pieces[0].shape[1]
    part = out.shape[1] // chunks
    copies = []
    for j in range(chunks):
        span = slice(j * part, (j + 1) * part)
        value = joined(order, width, pieces, dense, span)
        staged[:, span] = (begun[:, span] + value) * inverse[:, span]
        copies.append(pltpu.make_async_copy(staged.at[:, span], out.at[:, span], sems.at[j]))
        copies[-1].start()
    for copy in copies:
        copy.wait()


def results(order, begun, dense, inverse, pieces):
    rows, virtuals = begun.shape
    chunks = 6 if virtuals % 768 == 0 else 1
    vmem = pl.BlockSpec(memory_space=pltpu.VMEM)
    return pl.pallas_call(
        functools.partial(result_kernel, order, chunks),
        out_shape=jax.ShapeDtypeStruct((rows, virtuals), F32),
        in_specs=[vmem] * (3 + len(pieces)),
        out_specs=pl.BlockSpec(memory_space=pl.ANY),
        scratch_shapes=[
            pltpu.VMEM((rows, virtuals), F32),
            pltpu.SemaphoreType.DMA((chunks,)),
        ],
        compiler_params=pltpu.CompilerParams(vmem_limit_bytes=VMEM_LIMIT),
        name="results",
    )(begun, dense, inverse, *pieces)


def local(
    grids, pairs, amplitudes, packed_factor, screen, metric, occ_energy, vir_energy, pair_occ
):
    me = lax.axis_index("grid")
    pair = lax.axis_index("pair")
    place = me.astype(jnp.int32).reshape(1)
    order = [0] + list(range(grids - 1, 0, -1))
    rows = amplitudes.shape[1]
    tile = packed_factor.shape[1] // screen.shape[1]

    part, sent = keep(packed_factor)[None], packed_factor[None]
    step = 2
    while step < pairs:
        other = exchange(sent, "pair", pairs, step)
        part = jnp.where(
            pair & step == 0,
            jnp.concatenate([part, other], 0),
            jnp.concatenate([other, part], 0),
        )
        sent = part
        step *= 2
        ready, part = lax.optimization_barrier((place, part))
    parts = [exchange(part, "grid", grids, k) if k else part for k in range(grids)]
    packs = pack(ready, screen, amplitudes[0], tile)
    def swapped(part):
        other = exchange(part, "pair", pairs, 1)
        both = jnp.where(
            pair & 1 == 0, jnp.stack([part, other], 1), jnp.stack([other, part], 1)
        )
        return both.reshape(-1, packed_factor.shape[1])

    packs = list(packs)
    blocks = [None] * grids
    for k in order[1:]:
        part, packs[k] = lax.optimization_barrier((parts[k], packs[k]))
        blocks[k] = swapped(part)
    halves = []
    for ks in (order[1:2], order[2:]):
        group = half_products([packs[k] for k in ks], [blocks[k] for k in ks])
        if not halves:
            parts[0], group = lax.optimization_barrier((parts[0], group))
            packs[order[2]], parts[0] = lax.optimization_barrier((packs[order[2]], parts[0]))
        halves += [exchange(half, "grid", grids, k) for k, half in zip(ks, group)]
    blocks[0] = swapped(parts[0])
    halves = list(half_products([packs[0]], [blocks[0]])) + halves
    vir_energy, halves[0] = lax.optimization_barrier((vir_energy, halves[0]))
    own_vir = lax.dynamic_slice_in_dim(vir_energy, me * rows, rows, 0)[:, None]
    dense, turned, scale, inverse = prepare(
        place, screen, pair_occ, occ_energy, blocks, metric, own_vir, vir_energy[None, :], tile
    )
    early = grids // 2
    mixed = mixed_sum(order[:early], place, turned, halves[:early])
    sent = ladders(order, order[early:], turned, scale, mixed, halves[early:])
    pieces = [exchange(sent[k], "grid", grids, k) if k else sent[k] for k in order]
    begun = result_start(order[:early], dense, pieces[:early])
    return results(order[early:], begun, dense, inverse, pieces[early:])[None]


def solution(mesh):
    in_specs = (
        P("pair", "grid", None),
        P(("grid", "pair"), None),
        P(),
        P(None, "grid"),
        P(),
        P(),
        P("pair", None),
    )
    return jax.shard_map(
        functools.partial(local, mesh.shape["grid"], mesh.shape["pair"]),
        mesh=mesh,
        in_specs=in_specs,
        out_specs=P("pair", "grid", None),
        check_vma=False,
    )
```

```python
import functools

import jax
import jax.numpy as jnp
from jax import lax
from jax.experimental import pallas as pl
from jax.experimental.pallas import tpu as pltpu
from jax.sharding import PartitionSpec as P

BF16 = jnp.bfloat16
F32 = jnp.float32
VMEM_LIMIT = 40 * 1024 * 1024


def exchange(value, axis, size, step):
    return lax.ppermute(value, axis, [(i, i ^ step) for i in range(size)])


def keep_kernel(value, out):
    out[...] = value[...]


def keep(value):
    vmem = pl.BlockSpec(memory_space=pltpu.VMEM)
    return pl.pallas_call(
        keep_kernel,
        out_shape=pltpu.VMEM(value.shape, value.dtype),
        in_specs=[vmem],
        out_specs=vmem,
        name="keep",
    )(value)


def pack_kernel(tile, slots, count, place, screen, amplitudes, *rest):
    outs, sems = rest[:count], rest[count]
    copies = []
    for k in range(count):
        block = place[0] ^ k
        for s in range(slots):
            column = pl.multiple_of(screen[block, s] * tile, tile)
            copies.append(
                pltpu.make_async_copy(
                    amplitudes.at[:, pl.ds(column, tile)],
                    outs[k].at[:, pl.ds(s * tile, tile)],
                    sems.at[k * slots + s],
                )
            )
    for copy in copies:
        copy.start()
    for copy in copies:
        copy.wait()


def pack(place, screen, amplitudes, tile):
    rows = amplitudes.shape[0]
    count, slots = screen.shape
    smem = pl.BlockSpec(memory_space=pltpu.SMEM)
    hbm = pl.BlockSpec(memory_space=pltpu.HBM)
    return pl.pallas_call(
        functools.partial(pack_kernel, tile, slots, count),
        out_shape=[jax.ShapeDtypeStruct((rows, slots * tile), BF16)] * count,
        in_specs=[smem] * 2 + [hbm],
        out_specs=[pl.BlockSpec(memory_space=pltpu.VMEM)] * count,
        scratch_shapes=[pltpu.SemaphoreType.DMA((count * slots,))],
        cost_estimate=pl.CostEstimate(
            flops=0, bytes_accessed=4 * count * rows * slots * tile, transcendentals=0
        ),
        compiler_params=pltpu.CompilerParams(vmem_limit_bytes=VMEM_LIMIT),
        name="pack",
    )(place, screen, amplitudes)


def half_kernel(count, *refs):
    for k in range(count):
        refs[2 * count + k][...] = lax.dot_general(
            refs[k][...],
            refs[count + k][...],
            (((1,), (1,)), ((), ())),
            preferred_element_type=F32,
        ).astype(BF16)


def half_products(listed, blocks):
    count = len(listed)
    rows, columns = listed[0].shape
    width = blocks[0].shape[0]
    vmem = pl.BlockSpec(memory_space=pltpu.VMEM)
    return pl.pallas_call(
        functools.partial(half_kernel, count),
        out_shape=[jax.ShapeDtypeStruct((rows, width), BF16)] * count,
        in_specs=[vmem] * (2 * count),
        out_specs=[vmem] * count,
        cost_estimate=pl.CostEstimate(
            flops=2 * count * rows * columns * width, bytes_accessed=0, transcendentals=0
        ),
        compiler_params=pltpu.CompilerParams(vmem_limit_bytes=VMEM_LIMIT),
        name="half_products",
    )(*listed, *blocks)


def prepare_kernel(tile, slots, count, place, screen, pair_occ, occ_energy, *rest):
    blocks = rest[:count]
    metric, own_vir, vir, dense, turned, scale, inverse = rest[count:]
    width = blocks[0].shape[0]
    dense[...] = jnp.zeros_like(dense)
    turned[...] = jnp.zeros_like(turned)
    for k in range(count):
        b = place[0] ^ k
        span = slice(k * width, (k + 1) * width)
        block = blocks[k][...]
        other = block.T
        for s in range(slots):
            start = pl.multiple_of(screen[b, s] * tile, tile)
            dense[span, pl.ds(start, tile)] = block[:, s * tile : (s + 1) * tile]
            turned[pl.ds(start, tile), span] = other[s * tile : (s + 1) * tile, :]
        scale[:, span] = metric[pl.ds(pl.multiple_of(b * width, width), width), :].astype(F32).T
    occ_total = occ_energy[pair_occ[0, 0]] + occ_energy[pair_occ[0, 1]]
    inverse[...] = 1.0 / ((own_vir[...] + vir[...]) - occ_total)


def prepare(place, screen, pair_occ, occ_energy, blocks, metric, own_vir, vir, tile):
    count, slots = screen.shape
    points = count * blocks[0].shape[0]
    rows, virtuals = own_vir.shape[0], vir.shape[1]
    smem = pl.BlockSpec(memory_space=pltpu.SMEM)
    vmem = pl.BlockSpec(memory_space=pltpu.VMEM)
    return pl.pallas_call(
        functools.partial(prepare_kernel, tile, slots, count),
        out_shape=[
            jax.ShapeDtypeStruct((points, virtuals), BF16),
            jax.ShapeDtypeStruct((virtuals, points), BF16),
            jax.ShapeDtypeStruct((metric.shape[1], points), F32),
            jax.ShapeDtypeStruct((rows, virtuals), F32),
        ],
        in_specs=[smem] * 4 + [vmem] * (3 + count),
        out_specs=[vmem] * 4,
        cost_estimate=pl.CostEstimate(
            flops=0, bytes_accessed=8 * points * virtuals, transcendentals=0
        ),
        compiler_params=pltpu.CompilerParams(vmem_limit_bytes=VMEM_LIMIT),
        name="prepare",
    )(place, screen, pair_occ, occ_energy, *blocks, metric, own_vir, vir)


def mixed_part(half, factor):
    return lax.dot_general(half, factor, (((0,), (0,)), ((), ())), preferred_element_type=F32)


def mixed_kernel(order, place, turned, *rest):
    halves, out = rest[:-1], rest[-1]
    rows = halves[0].shape[0]
    total = None
    for k, half in zip(order, halves):
        start = pl.multiple_of((place[0] ^ k) * rows, rows)
        part = mixed_part(half[...], turned[pl.ds(start, rows), :])
        total = part if total is None else total + part
    out[...] = total


def mixed_sum(order, place, turned, halves):
    known = len(halves)
    width, points = halves[0].shape[1], turned.shape[1]
    vmem = pl.BlockSpec(memory_space=pltpu.VMEM)
    return pl.pallas_call(
        functools.partial(mixed_kernel, order),
        out_shape=jax.ShapeDtypeStruct((width, points), F32),
        in_specs=[pl.BlockSpec(memory_space=pltpu.SMEM)] + [vmem] * (1 + known),
        out_specs=vmem,
        cost_estimate=pl.CostEstimate(
            flops=2 * known * halves[0].size * points, bytes_accessed=0, transcendentals=0
        ),
        compiler_params=pltpu.CompilerParams(vmem_limit_bytes=VMEM_LIMIT),
        name="mixed",
    )(place, turned, *halves)


def own_rows(turned, k, rows):
    start = (lax.axis_index("grid") ^ k) * rows
    return turned[pl.ds(pl.multiple_of(start, rows), rows), :]


def ladder_piece(turned, k, weighted, rows):
    return lax.dot_general(
        own_rows(turned, k, rows), weighted, (((1,), (1,)), ((), ())), preferred_element_type=F32
    ).astype(BF16)


def weighted_kernel(first, late, turned, scale, mixed, *rest):
    halves, (weighted, out) = rest[: len(late)], rest[len(late) :]
    rows = halves[0].shape[0]
    total = mixed[...]
    for k, half in zip(late, halves):
        total = total + mixed_part(half[...], own_rows(turned, k, rows))
    weighted[...] = (scale[...] * total).astype(BF16)
    out[...] = ladder_piece(turned, first, weighted[...], rows)


def ladder_kernel(ks, turned, weighted, *outs):
    for k, out in zip(ks, outs):
        out[...] = ladder_piece(turned, k, weighted[...], out.shape[0])


def ladders(order, late, turned, scale, mixed, halves):
    rows, width = halves[0].shape
    vmem = pl.BlockSpec(memory_space=pltpu.VMEM)
    piece = jax.ShapeDtypeStruct((rows, width), BF16)
    limit = pltpu.CompilerParams(vmem_limit_bytes=VMEM_LIMIT)
    pieces = {}
    weighted, pieces[order[1]] = pl.pallas_call(
        functools.partial(weighted_kernel, order[1], late),
        out_shape=[jax.ShapeDtypeStruct(scale.shape, BF16), piece],
        in_specs=[vmem] * (3 + len(halves)),
        out_specs=[vmem] * 2,
        compiler_params=limit,
        name="weighted",
    )(turned, scale, mixed, *halves)
    for ks in (order[2:], order[:1]):
        outs = pl.pallas_call(
            functools.partial(ladder_kernel, ks),
            out_shape=[piece] * len(ks),
            in_specs=[vmem] * 2,
            out_specs=[vmem] * len(ks),
            cost_estimate=pl.CostEstimate(
                flops=2 * len(ks) * rows * weighted.size, bytes_accessed=0, transcendentals=0
            ),
            compiler_params=limit,
            name="ladders",
        )(turned, weighted)
        pieces.update(zip(ks, outs))
    return [pieces[k] for k in range(len(order))]


def joined(order, width, pieces, dense, span):
    total = None
    for k, piece in zip(order, pieces):
        block = dense[k * width : (k + 1) * width, span]
        part = jnp.dot(piece[...], block, preferred_element_type=F32)
        total = part if total is None else total + part
    return total


def start_kernel(order, dense, *rest):
    pieces, out = rest[:-1], rest[-1]
    out[...] = joined(order, pieces[0].shape[1], pieces, dense, slice(None))


def result_start(order, dense, pieces):
    rows, width = pieces[0].shape
    vmem = pl.BlockSpec(memory_space=pltpu.VMEM)
    return pl.pallas_call(
        functools.partial(start_kernel, order),
        out_shape=jax.ShapeDtypeStruct((rows, dense.shape[1]), F32),
        in_specs=[vmem] * (1 + len(pieces)),
        out_specs=vmem,
        cost_estimate=pl.CostEstimate(
            flops=2 * len(pieces) * rows * width * dense.shape[1],
            bytes_accessed=0,
            transcendentals=0,
        ),
        compiler_params=pltpu.CompilerParams(vmem_limit_bytes=VMEM_LIMIT),
        name="result_start",
    )(dense, *pieces)


def result_kernel(order, chunks, begun, dense, inverse, *rest):
    *pieces, out, staged, sems = rest
    width = pieces[0].shape[1]
    part = out.shape[1] // chunks
    copies = []
    for j in range(chunks):
        span = slice(j * part, (j + 1) * part)
        value = joined(order, width, pieces, dense, span)
        staged[:, span] = (begun[:, span] + value) * inverse[:, span]
        copies.append(pltpu.make_async_copy(staged.at[:, span], out.at[:, span], sems.at[j]))
        copies[-1].start()
    for copy in copies:
        copy.wait()


def results(order, begun, dense, inverse, pieces):
    rows, virtuals = begun.shape
    chunks = 3 if virtuals % 768 == 0 else 1
    vmem = pl.BlockSpec(memory_space=pltpu.VMEM)
    return pl.pallas_call(
        functools.partial(result_kernel, order, chunks),
        out_shape=jax.ShapeDtypeStruct((rows, virtuals), F32),
        in_specs=[vmem] * (3 + len(pieces)),
        out_specs=pl.BlockSpec(memory_space=pl.ANY),
        scratch_shapes=[
            pltpu.VMEM((rows, virtuals), F32),
            pltpu.SemaphoreType.DMA((chunks,)),
        ],
        compiler_params=pltpu.CompilerParams(vmem_limit_bytes=VMEM_LIMIT),
        name="results",
    )(begun, dense, inverse, *pieces)


def local(
    grids, pairs, amplitudes, packed_factor, screen, metric, occ_energy, vir_energy, pair_occ
):
    me = lax.axis_index("grid")
    pair = lax.axis_index("pair")
    place = me.astype(jnp.int32).reshape(1)
    order = [0] + list(range(grids - 1, 0, -1))
    rows = amplitudes.shape[1]
    tile = packed_factor.shape[1] // screen.shape[1]

    part, sent = keep(packed_factor)[None], packed_factor[None]
    step = 2
    while step < pairs:
        other = exchange(sent, "pair", pairs, step)
        part = jnp.where(
            pair & step == 0,
            jnp.concatenate([part, other], 0),
            jnp.concatenate([other, part], 0),
        )
        sent = part
        step *= 2
        ready, part = lax.optimization_barrier((place, part))
    parts = [exchange(part, "grid", grids, k) if k else part for k in range(grids)]
    packs = pack(ready, screen, amplitudes[0], tile)
    def swapped(part):
        other = exchange(part, "pair", pairs, 1)
        both = jnp.where(
            pair & 1 == 0, jnp.stack([part, other], 1), jnp.stack([other, part], 1)
        )
        return both.reshape(-1, packed_factor.shape[1])

    packs = list(packs)
    blocks = [None] * grids
    for k in order[1:]:
        part, packs[k] = lax.optimization_barrier((parts[k], packs[k]))
        blocks[k] = swapped(part)
    halves = []
    for ks in (order[1:2], order[2:]):
        group = half_products([packs[k] for k in ks], [blocks[k] for k in ks])
        if not halves:
            parts[0], group = lax.optimization_barrier((parts[0], group))
        halves += [exchange(half, "grid", grids, k) for k, half in zip(ks, group)]
    blocks[0] = swapped(parts[0])
    halves = list(half_products([packs[0]], [blocks[0]])) + halves
    vir_energy, halves[0] = lax.optimization_barrier((vir_energy, halves[0]))
    own_vir = lax.dynamic_slice_in_dim(vir_energy, me * rows, rows, 0)[:, None]
    dense, turned, scale, inverse = prepare(
        place, screen, pair_occ, occ_energy, blocks, metric, own_vir, vir_energy[None, :], tile
    )
    early = grids // 2
    mixed = mixed_sum(order[:early], place, turned, halves[:early])
    sent = ladders(order, order[early:], turned, scale, mixed, halves[early:])
    pieces = [exchange(sent[k], "grid", grids, k) if k else sent[k] for k in order]
    begun = result_start(order[:early], dense, pieces[:early])
    return results(order[early:], begun, dense, inverse, pieces[early:])[None]


def solution(mesh):
    in_specs = (
        P("pair", "grid", None),
        P(("grid", "pair"), None),
        P(),
        P(None, "grid"),
        P(),
        P(),
        P("pair", None),
    )
    return jax.shard_map(
        functools.partial(local, mesh.shape["grid"], mesh.shape["pair"]),
        mesh=mesh,
        in_specs=in_specs,
        out_specs=P("pair", "grid", None),
        check_vma=False,
    )
```

```python
import functools

import jax
import jax.numpy as jnp
from jax import lax
from jax.experimental import pallas as pl
from jax.experimental.pallas import tpu as pltpu
from jax.sharding import PartitionSpec as P

BF16 = jnp.bfloat16
F32 = jnp.float32
VMEM_LIMIT = 40 * 1024 * 1024


def exchange(value, axis, size, step):
    return lax.ppermute(value, axis, [(i, i ^ step) for i in range(size)])


def keep_kernel(value, out):
    out[...] = value[...]


def keep(value):
    vmem = pl.BlockSpec(memory_space=pltpu.VMEM)
    return pl.pallas_call(
        keep_kernel,
        out_shape=pltpu.VMEM(value.shape, value.dtype),
        in_specs=[vmem],
        out_specs=vmem,
        name="keep",
    )(value)


def pack_kernel(tile, slots, count, place, screen, amplitudes, *rest):
    outs, sems = rest[:count], rest[count]
    copies = []
    for k in range(count):
        block = place[0] ^ k
        for s in range(slots):
            column = pl.multiple_of(screen[block, s] * tile, tile)
            copies.append(
                pltpu.make_async_copy(
                    amplitudes.at[:, pl.ds(column, tile)],
                    outs[k].at[:, pl.ds(s * tile, tile)],
                    sems.at[k * slots + s],
                )
            )
    for copy in copies:
        copy.start()
    for copy in copies:
        copy.wait()


def pack(place, screen, amplitudes, tile):
    rows = amplitudes.shape[0]
    count, slots = screen.shape
    smem = pl.BlockSpec(memory_space=pltpu.SMEM)
    hbm = pl.BlockSpec(memory_space=pltpu.HBM)
    return pl.pallas_call(
        functools.partial(pack_kernel, tile, slots, count),
        out_shape=[jax.ShapeDtypeStruct((rows, slots * tile), BF16)] * count,
        in_specs=[smem] * 2 + [hbm],
        out_specs=[pl.BlockSpec(memory_space=pltpu.VMEM)] * count,
        scratch_shapes=[pltpu.SemaphoreType.DMA((count * slots,))],
        cost_estimate=pl.CostEstimate(
            flops=0, bytes_accessed=4 * count * rows * slots * tile, transcendentals=0
        ),
        compiler_params=pltpu.CompilerParams(vmem_limit_bytes=VMEM_LIMIT),
        name="pack",
    )(place, screen, amplitudes)


def half_kernel(count, *refs):
    for k in range(count):
        refs[2 * count + k][...] = lax.dot_general(
            refs[count + k][...],
            refs[k][...],
            (((1,), (1,)), ((), ())),
            preferred_element_type=F32,
        ).astype(BF16)


def half_products(listed, blocks):
    count = len(listed)
    rows, columns = listed[0].shape
    width = blocks[0].shape[0]
    vmem = pl.BlockSpec(memory_space=pltpu.VMEM)
    return pl.pallas_call(
        functools.partial(half_kernel, count),
        out_shape=[jax.ShapeDtypeStruct((width, rows), BF16)] * count,
        in_specs=[vmem] * (2 * count),
        out_specs=[vmem] * count,
        cost_estimate=pl.CostEstimate(
            flops=2 * count * rows * columns * width, bytes_accessed=0, transcendentals=0
        ),
        compiler_params=pltpu.CompilerParams(vmem_limit_bytes=VMEM_LIMIT),
        name="half_products",
    )(*listed, *blocks)


def prepare_kernel(tile, slots, count, place, screen, pair_occ, occ_energy, *rest):
    blocks = rest[:count]
    metric, own_vir, vir, dense, turned, scale, inverse = rest[count:]
    width = blocks[0].shape[0]
    dense[...] = jnp.zeros_like(dense)
    turned[...] = jnp.zeros_like(turned)
    for k in range(count):
        b = place[0] ^ k
        span = slice(k * width, (k + 1) * width)
        block = blocks[k][...]
        other = block.T
        for s in range(slots):
            start = pl.multiple_of(screen[b, s] * tile, tile)
            dense[span, pl.ds(start, tile)] = block[:, s * tile : (s + 1) * tile]
            turned[pl.ds(start, tile), span] = other[s * tile : (s + 1) * tile, :]
        scale[:, span] = metric[pl.ds(pl.multiple_of(b * width, width), width), :].astype(F32).T
    occ_total = occ_energy[pair_occ[0, 0]] + occ_energy[pair_occ[0, 1]]
    inverse[...] = 1.0 / ((own_vir[...] + vir[...]) - occ_total)


def prepare(place, screen, pair_occ, occ_energy, blocks, metric, own_vir, vir, tile):
    count, slots = screen.shape
    points = count * blocks[0].shape[0]
    rows, virtuals = own_vir.shape[0], vir.shape[1]
    smem = pl.BlockSpec(memory_space=pltpu.SMEM)
    vmem = pl.BlockSpec(memory_space=pltpu.VMEM)
    return pl.pallas_call(
        functools.partial(prepare_kernel, tile, slots, count),
        out_shape=[
            jax.ShapeDtypeStruct((points, virtuals), BF16),
            jax.ShapeDtypeStruct((virtuals, points), BF16),
            jax.ShapeDtypeStruct((metric.shape[1], points), F32),
            jax.ShapeDtypeStruct((rows, virtuals), F32),
        ],
        in_specs=[smem] * 4 + [vmem] * (3 + count),
        out_specs=[vmem] * 4,
        cost_estimate=pl.CostEstimate(
            flops=0, bytes_accessed=8 * points * virtuals, transcendentals=0
        ),
        compiler_params=pltpu.CompilerParams(vmem_limit_bytes=VMEM_LIMIT),
        name="prepare",
    )(place, screen, pair_occ, occ_energy, *blocks, metric, own_vir, vir)


def mixed_part(half, factor):
    return jnp.dot(half, factor, preferred_element_type=F32)


def mixed_kernel(order, place, turned, *rest):
    halves, out = rest[:-1], rest[-1]
    rows = halves[0].shape[1]
    total = None
    for k, half in zip(order, halves):
        start = pl.multiple_of((place[0] ^ k) * rows, rows)
        part = mixed_part(half[...], turned[pl.ds(start, rows), :])
        total = part if total is None else total + part
    out[...] = total


def mixed_sum(order, place, turned, halves):
    known = len(halves)
    width, points = halves[0].shape[0], turned.shape[1]
    vmem = pl.BlockSpec(memory_space=pltpu.VMEM)
    return pl.pallas_call(
        functools.partial(mixed_kernel, order),
        out_shape=jax.ShapeDtypeStruct((width, points), F32),
        in_specs=[pl.BlockSpec(memory_space=pltpu.SMEM)] + [vmem] * (1 + known),
        out_specs=vmem,
        cost_estimate=pl.CostEstimate(
            flops=2 * known * halves[0].size * points, bytes_accessed=0, transcendentals=0
        ),
        compiler_params=pltpu.CompilerParams(vmem_limit_bytes=VMEM_LIMIT),
        name="mixed",
    )(place, turned, *halves)


def own_rows(turned, k, rows):
    start = (lax.axis_index("grid") ^ k) * rows
    return turned[pl.ds(pl.multiple_of(start, rows), rows), :]


def ladder_piece(turned, k, weighted, rows):
    return lax.dot_general(
        own_rows(turned, k, rows), weighted, (((1,), (1,)), ((), ())), preferred_element_type=F32
    ).astype(BF16)


def weighted_kernel(first, late, turned, scale, mixed, *rest):
    halves, (weighted, out) = rest[: len(late)], rest[len(late) :]
    rows = halves[0].shape[1]
    total = mixed[...]
    for k, half in zip(late, halves):
        total = total + mixed_part(half[...], own_rows(turned, k, rows))
    weighted[...] = (scale[...] * total).astype(BF16)
    out[...] = ladder_piece(turned, first, weighted[...], rows)


def ladder_kernel(ks, turned, weighted, *outs):
    for k, out in zip(ks, outs):
        out[...] = ladder_piece(turned, k, weighted[...], out.shape[0])


def ladders(order, late, turned, scale, mixed, halves):
    width, rows = halves[0].shape
    vmem = pl.BlockSpec(memory_space=pltpu.VMEM)
    piece = jax.ShapeDtypeStruct((rows, width), BF16)
    limit = pltpu.CompilerParams(vmem_limit_bytes=VMEM_LIMIT)
    pieces = {}
    weighted, pieces[order[1]] = pl.pallas_call(
        functools.partial(weighted_kernel, order[1], late),
        out_shape=[jax.ShapeDtypeStruct(scale.shape, BF16), piece],
        in_specs=[vmem] * (3 + len(halves)),
        out_specs=[vmem] * 2,
        compiler_params=limit,
        name="weighted",
    )(turned, scale, mixed, *halves)
    for ks in (order[2:], order[:1]):
        outs = pl.pallas_call(
            functools.partial(ladder_kernel, ks),
            out_shape=[piece] * len(ks),
            in_specs=[vmem] * 2,
            out_specs=[vmem] * len(ks),
            cost_estimate=pl.CostEstimate(
                flops=2 * len(ks) * rows * weighted.size, bytes_accessed=0, transcendentals=0
            ),
            compiler_params=limit,
            name="ladders",
        )(turned, weighted)
        pieces.update(zip(ks, outs))
    return [pieces[k] for k in range(len(order))]


def joined(order, width, pieces, dense, span):
    total = None
    for k, piece in zip(order, pieces):
        block = dense[k * width : (k + 1) * width, span]
        part = jnp.dot(piece[...], block, preferred_element_type=F32)
        total = part if total is None else total + part
    return total


def start_kernel(order, dense, *rest):
    pieces, out = rest[:-1], rest[-1]
    out[...] = joined(order, pieces[0].shape[1], pieces, dense, slice(None))


def result_start(order, dense, pieces):
    rows, width = pieces[0].shape
    vmem = pl.BlockSpec(memory_space=pltpu.VMEM)
    return pl.pallas_call(
        functools.partial(start_kernel, order),
        out_shape=jax.ShapeDtypeStruct((rows, dense.shape[1]), F32),
        in_specs=[vmem] * (1 + len(pieces)),
        out_specs=vmem,
        cost_estimate=pl.CostEstimate(
            flops=2 * len(pieces) * rows * width * dense.shape[1],
            bytes_accessed=0,
            transcendentals=0,
        ),
        compiler_params=pltpu.CompilerParams(vmem_limit_bytes=VMEM_LIMIT),
        name="result_start",
    )(dense, *pieces)


def result_kernel(order, chunks, begun, dense, inverse, *rest):
    *pieces, out, staged, sems = rest
    width = pieces[0].shape[1]
    part = out.shape[1] // chunks
    copies = []
    for j in range(chunks):
        span = slice(j * part, (j + 1) * part)
        value = joined(order, width, pieces, dense, span)
        staged[:, span] = (begun[:, span] + value) * inverse[:, span]
        copies.append(pltpu.make_async_copy(staged.at[:, span], out.at[:, span], sems.at[j]))
        copies[-1].start()
    for copy in copies:
        copy.wait()


def results(order, begun, dense, inverse, pieces):
    rows, virtuals = begun.shape
    chunks = 3 if virtuals % 768 == 0 else 1
    vmem = pl.BlockSpec(memory_space=pltpu.VMEM)
    return pl.pallas_call(
        functools.partial(result_kernel, order, chunks),
        out_shape=jax.ShapeDtypeStruct((rows, virtuals), F32),
        in_specs=[vmem] * (3 + len(pieces)),
        out_specs=pl.BlockSpec(memory_space=pl.ANY),
        scratch_shapes=[
            pltpu.VMEM((rows, virtuals), F32),
            pltpu.SemaphoreType.DMA((chunks,)),
        ],
        compiler_params=pltpu.CompilerParams(vmem_limit_bytes=VMEM_LIMIT),
        name="results",
    )(begun, dense, inverse, *pieces)


def local(
    grids, pairs, amplitudes, packed_factor, screen, metric, occ_energy, vir_energy, pair_occ
):
    me = lax.axis_index("grid")
    pair = lax.axis_index("pair")
    place = me.astype(jnp.int32).reshape(1)
    order = [0] + list(range(grids - 1, 0, -1))
    rows = amplitudes.shape[1]
    tile = packed_factor.shape[1] // screen.shape[1]

    part, sent = keep(packed_factor)[None], packed_factor[None]
    step = 2
    while step < pairs:
        other = exchange(sent, "pair", pairs, step)
        part = jnp.where(
            pair & step == 0,
            jnp.concatenate([part, other], 0),
            jnp.concatenate([other, part], 0),
        )
        sent = part
        step *= 2
        ready, part = lax.optimization_barrier((place, part))
    parts = [exchange(part, "grid", grids, k) if k else part for k in range(grids)]
    packs = pack(ready, screen, amplitudes[0], tile)
    def swapped(part):
        other = exchange(part, "pair", pairs, 1)
        both = jnp.where(
            pair & 1 == 0, jnp.stack([part, other], 1), jnp.stack([other, part], 1)
        )
        return both.reshape(-1, packed_factor.shape[1])

    packs = list(packs)
    blocks = [None] * grids
    for k in order[1:]:
        part, packs[k] = lax.optimization_barrier((parts[k], packs[k]))
        blocks[k] = swapped(part)
    halves = []
    for ks in (order[1:2], order[2:]):
        group = half_products([packs[k] for k in ks], [blocks[k] for k in ks])
        if not halves:
            parts[0], group = lax.optimization_barrier((parts[0], group))
        halves += [exchange(half, "grid", grids, k) for k, half in zip(ks, group)]
    blocks[0] = swapped(parts[0])
    halves = list(half_products([packs[0]], [blocks[0]])) + halves
    vir_energy, halves[0] = lax.optimization_barrier((vir_energy, halves[0]))
    own_vir = lax.dynamic_slice_in_dim(vir_energy, me * rows, rows, 0)[:, None]
    dense, turned, scale, inverse = prepare(
        place, screen, pair_occ, occ_energy, blocks, metric, own_vir, vir_energy[None, :], tile
    )
    early = grids // 2
    mixed = mixed_sum(order[:early], place, turned, halves[:early])
    sent = ladders(order, order[early:], turned, scale, mixed, halves[early:])
    pieces = [exchange(sent[k], "grid", grids, k) if k else sent[k] for k in order]
    begun = result_start(order[:early], dense, pieces[:early])
    return results(order[early:], begun, dense, inverse, pieces[early:])[None]


def solution(mesh):
    in_specs = (
        P("pair", "grid", None),
        P(("grid", "pair"), None),
        P(),
        P(None, "grid"),
        P(),
        P(),
        P("pair", None),
    )
    return jax.shard_map(
        functools.partial(local, mesh.shape["grid"], mesh.shape["pair"]),
        mesh=mesh,
        in_specs=in_specs,
        out_specs=P("pair", "grid", None),
        check_vma=False,
    )
```

```python
import functools

import jax
import jax.numpy as jnp
from jax import lax
from jax.experimental import pallas as pl
from jax.experimental.pallas import tpu as pltpu
from jax.sharding import PartitionSpec as P

BF16 = jnp.bfloat16
F32 = jnp.float32
VMEM_LIMIT = 40 * 1024 * 1024


def exchange(value, axis, size, step):
    return lax.ppermute(value, axis, [(i, i ^ step) for i in range(size)])


def keep_kernel(value, out):
    out[...] = value[...]


def keep(value):
    vmem = pl.BlockSpec(memory_space=pltpu.VMEM)
    return pl.pallas_call(
        keep_kernel,
        out_shape=pltpu.VMEM(value.shape, value.dtype),
        in_specs=[vmem],
        out_specs=vmem,
        name="keep",
    )(value)


def pack_kernel(tile, slots, count, place, screen, amplitudes, *rest):
    outs, sems = rest[:count], rest[count]
    copies = []
    for k in range(count):
        block = place[0] ^ k
        for s in range(slots):
            column = pl.multiple_of(screen[block, s] * tile, tile)
            copies.append(
                pltpu.make_async_copy(
                    amplitudes.at[:, pl.ds(column, tile)],
                    outs[k].at[:, pl.ds(s * tile, tile)],
                    sems.at[k * slots + s],
                )
            )
    for copy in copies:
        copy.start()
    for copy in copies:
        copy.wait()


def pack(place, screen, amplitudes, tile):
    rows = amplitudes.shape[0]
    count, slots = screen.shape
    smem = pl.BlockSpec(memory_space=pltpu.SMEM)
    hbm = pl.BlockSpec(memory_space=pltpu.HBM)
    return pl.pallas_call(
        functools.partial(pack_kernel, tile, slots, count),
        out_shape=[jax.ShapeDtypeStruct((rows, slots * tile), BF16)] * count,
        in_specs=[smem] * 2 + [hbm],
        out_specs=[pl.BlockSpec(memory_space=pltpu.VMEM)] * count,
        scratch_shapes=[pltpu.SemaphoreType.DMA((count * slots,))],
        cost_estimate=pl.CostEstimate(
            flops=0, bytes_accessed=4 * count * rows * slots * tile, transcendentals=0
        ),
        compiler_params=pltpu.CompilerParams(vmem_limit_bytes=VMEM_LIMIT),
        name="pack",
    )(place, screen, amplitudes)


def half_kernel(count, *refs):
    for k in range(count):
        refs[2 * count + k][...] = lax.dot_general(
            refs[count + k][...],
            refs[k][...],
            (((1,), (1,)), ((), ())),
            preferred_element_type=F32,
        ).astype(BF16)


def half_products(listed, blocks):
    count = len(listed)
    rows, columns = listed[0].shape
    width = blocks[0].shape[0]
    vmem = pl.BlockSpec(memory_space=pltpu.VMEM)
    return pl.pallas_call(
        functools.partial(half_kernel, count),
        out_shape=[jax.ShapeDtypeStruct((width, rows), BF16)] * count,
        in_specs=[vmem] * (2 * count),
        out_specs=[vmem] * count,
        cost_estimate=pl.CostEstimate(
            flops=2 * count * rows * columns * width, bytes_accessed=0, transcendentals=0
        ),
        compiler_params=pltpu.CompilerParams(vmem_limit_bytes=VMEM_LIMIT),
        name="half_products",
    )(*listed, *blocks)


def prepare_kernel(tile, slots, count, place, screen, pair_occ, occ_energy, *rest):
    blocks = rest[:count]
    metric, own_vir, vir, dense, turned, scale, inverse = rest[count:]
    width = blocks[0].shape[0]
    dense[...] = jnp.zeros_like(dense)
    turned[...] = jnp.zeros_like(turned)
    for k in range(count):
        b = place[0] ^ k
        span = slice(k * width, (k + 1) * width)
        block = blocks[k][...]
        other = block.T
        for s in range(slots):
            start = pl.multiple_of(screen[b, s] * tile, tile)
            dense[span, pl.ds(start, tile)] = block[:, s * tile : (s + 1) * tile]
            turned[pl.ds(start, tile), span] = other[s * tile : (s + 1) * tile, :]
        scale[:, span] = metric[pl.ds(pl.multiple_of(b * width, width), width), :].astype(F32).T
    occ_total = occ_energy[pair_occ[0, 0]] + occ_energy[pair_occ[0, 1]]
    inverse[...] = 1.0 / ((own_vir[...] + vir[...]) - occ_total)


def prepare(place, screen, pair_occ, occ_energy, blocks, metric, own_vir, vir, tile):
    count, slots = screen.shape
    points = count * blocks[0].shape[0]
    rows, virtuals = own_vir.shape[0], vir.shape[1]
    smem = pl.BlockSpec(memory_space=pltpu.SMEM)
    vmem = pl.BlockSpec(memory_space=pltpu.VMEM)
    return pl.pallas_call(
        functools.partial(prepare_kernel, tile, slots, count),
        out_shape=[
            jax.ShapeDtypeStruct((points, virtuals), BF16),
            jax.ShapeDtypeStruct((virtuals, points), BF16),
            jax.ShapeDtypeStruct((metric.shape[1], points), F32),
            jax.ShapeDtypeStruct((rows, virtuals), F32),
        ],
        in_specs=[smem] * 4 + [vmem] * (3 + count),
        out_specs=[vmem] * 4,
        cost_estimate=pl.CostEstimate(
            flops=0, bytes_accessed=8 * points * virtuals, transcendentals=0
        ),
        compiler_params=pltpu.CompilerParams(vmem_limit_bytes=VMEM_LIMIT),
        name="prepare",
    )(place, screen, pair_occ, occ_energy, *blocks, metric, own_vir, vir)


def mixed_part(half, factor):
    return jnp.dot(half, factor, preferred_element_type=F32)


def mixed_kernel(order, place, turned, *rest):
    halves, out = rest[:-1], rest[-1]
    rows = halves[0].shape[1]
    total = None
    for k, half in zip(order, halves):
        start = pl.multiple_of((place[0] ^ k) * rows, rows)
        part = mixed_part(half[...], turned[pl.ds(start, rows), :])
        total = part if total is None else total + part
    out[...] = total


def mixed_sum(order, place, turned, halves):
    known = len(halves)
    width, points = halves[0].shape[0], turned.shape[1]
    vmem = pl.BlockSpec(memory_space=pltpu.VMEM)
    return pl.pallas_call(
        functools.partial(mixed_kernel, order),
        out_shape=jax.ShapeDtypeStruct((width, points), F32),
        in_specs=[pl.BlockSpec(memory_space=pltpu.SMEM)] + [vmem] * (1 + known),
        out_specs=vmem,
        cost_estimate=pl.CostEstimate(
            flops=2 * known * halves[0].size * points, bytes_accessed=0, transcendentals=0
        ),
        compiler_params=pltpu.CompilerParams(vmem_limit_bytes=VMEM_LIMIT),
        name="mixed",
    )(place, turned, *halves)


def own_rows(turned, k, rows):
    start = (lax.axis_index("grid") ^ k) * rows
    return turned[pl.ds(pl.multiple_of(start, rows), rows), :]


def ladder_piece(turned, k, weighted, rows):
    return lax.dot_general(
        own_rows(turned, k, rows), weighted, (((1,), (1,)), ((), ())), preferred_element_type=F32
    ).astype(BF16)


def weighted_kernel(first, late, turned, scale, mixed, *rest):
    halves, (weighted, out) = rest[: len(late)], rest[len(late) :]
    rows = halves[0].shape[1]
    total = mixed[...]
    for k, half in zip(late, halves):
        total = total + mixed_part(half[...], own_rows(turned, k, rows))
    weighted[...] = (scale[...] * total).astype(BF16)
    out[...] = ladder_piece(turned, first, weighted[...], rows)


def ladder_kernel(ks, turned, weighted, *outs):
    for k, out in zip(ks, outs):
        out[...] = ladder_piece(turned, k, weighted[...], out.shape[0])


def ladders(order, late, turned, scale, mixed, halves):
    width, rows = halves[0].shape
    vmem = pl.BlockSpec(memory_space=pltpu.VMEM)
    piece = jax.ShapeDtypeStruct((rows, width), BF16)
    limit = pltpu.CompilerParams(vmem_limit_bytes=VMEM_LIMIT)
    pieces = {}
    weighted, pieces[order[1]] = pl.pallas_call(
        functools.partial(weighted_kernel, order[1], late),
        out_shape=[jax.ShapeDtypeStruct(scale.shape, BF16), piece],
        in_specs=[vmem] * (3 + len(halves)),
        out_specs=[vmem] * 2,
        compiler_params=limit,
        name="weighted",
    )(turned, scale, mixed, *halves)
    for ks in (order[2:], order[:1]):
        outs = pl.pallas_call(
            functools.partial(ladder_kernel, ks),
            out_shape=[piece] * len(ks),
            in_specs=[vmem] * 2,
            out_specs=[vmem] * len(ks),
            cost_estimate=pl.CostEstimate(
                flops=2 * len(ks) * rows * weighted.size, bytes_accessed=0, transcendentals=0
            ),
            compiler_params=limit,
            name="ladders",
        )(turned, weighted)
        pieces.update(zip(ks, outs))
    return [pieces[k] for k in range(len(order))]


def joined(order, width, pieces, dense, span):
    total = None
    for k, piece in zip(order, pieces):
        block = dense[k * width : (k + 1) * width, span]
        part = jnp.dot(piece[...], block, preferred_element_type=F32)
        total = part if total is None else total + part
    return total


def start_kernel(order, dense, *rest):
    pieces, out = rest[:-1], rest[-1]
    out[...] = joined(order, pieces[0].shape[1], pieces, dense, slice(None))


def result_start(order, dense, pieces):
    rows, width = pieces[0].shape
    vmem = pl.BlockSpec(memory_space=pltpu.VMEM)
    return pl.pallas_call(
        functools.partial(start_kernel, order),
        out_shape=jax.ShapeDtypeStruct((rows, dense.shape[1]), F32),
        in_specs=[vmem] * (1 + len(pieces)),
        out_specs=vmem,
        cost_estimate=pl.CostEstimate(
            flops=2 * len(pieces) * rows * width * dense.shape[1],
            bytes_accessed=0,
            transcendentals=0,
        ),
        compiler_params=pltpu.CompilerParams(vmem_limit_bytes=VMEM_LIMIT),
        name="result_start",
    )(dense, *pieces)


def result_kernel(order, chunks, begun, dense, inverse, *rest):
    *pieces, out, staged, sems = rest
    width = pieces[0].shape[1]
    part = out.shape[1] // chunks
    copies = []
    for j in range(chunks):
        span = slice(j * part, (j + 1) * part)
        value = joined(order, width, pieces, dense, span)
        staged[:, span] = (begun[:, span] + value) * inverse[:, span]
        copies.append(pltpu.make_async_copy(staged.at[:, span], out.at[:, span], sems.at[j]))
        copies[-1].start()
    for copy in copies:
        copy.wait()


def results(order, begun, dense, inverse, pieces):
    rows, virtuals = begun.shape
    chunks = 3 if virtuals % 768 == 0 else 1
    vmem = pl.BlockSpec(memory_space=pltpu.VMEM)
    return pl.pallas_call(
        functools.partial(result_kernel, order, chunks),
        out_shape=jax.ShapeDtypeStruct((rows, virtuals), F32),
        in_specs=[vmem] * (3 + len(pieces)),
        out_specs=pl.BlockSpec(memory_space=pl.ANY),
        scratch_shapes=[
            pltpu.VMEM((rows, virtuals), F32),
            pltpu.SemaphoreType.DMA((chunks,)),
        ],
        compiler_params=pltpu.CompilerParams(vmem_limit_bytes=VMEM_LIMIT),
        name="results",
    )(begun, dense, inverse, *pieces)


def local(
    grids, pairs, amplitudes, packed_factor, screen, metric, occ_energy, vir_energy, pair_occ
):
    me = lax.axis_index("grid")
    pair = lax.axis_index("pair")
    place = me.astype(jnp.int32).reshape(1)
    order = [0] + list(range(grids - 1, 0, -1))
    rows = amplitudes.shape[1]
    tile = packed_factor.shape[1] // screen.shape[1]

    part, sent = keep(packed_factor)[None], packed_factor[None]
    step = 2
    while step < pairs:
        other = exchange(sent, "pair", pairs, step)
        part = jnp.where(
            pair & step == 0,
            jnp.concatenate([part, other], 0),
            jnp.concatenate([other, part], 0),
        )
        sent = part
        step *= 2
        ready, part = lax.optimization_barrier((place, part))
    parts = [exchange(part, "grid", grids, k) if k else part for k in range(grids)]
    packs = pack(ready, screen, amplitudes[0], tile)
    def swapped(part):
        other = exchange(part, "pair", pairs, 1)
        both = jnp.where(
            pair & 1 == 0, jnp.stack([part, other], 1), jnp.stack([other, part], 1)
        )
        return both.reshape(-1, packed_factor.shape[1])

    packs = list(packs)
    blocks = [None] * grids
    for k in order[1:]:
        part, packs[k] = lax.optimization_barrier((parts[k], packs[k]))
        blocks[k] = swapped(part)
    halves = []
    for ks in (order[1:2], order[2:]):
        group = half_products([packs[k] for k in ks], [blocks[k] for k in ks])
        if not halves:
            parts[0], group = lax.optimization_barrier((parts[0], group))
            packs[order[2]], parts[0] = lax.optimization_barrier((packs[order[2]], parts[0]))
        halves += [exchange(half, "grid", grids, k) for k, half in zip(ks, group)]
    blocks[0] = swapped(parts[0])
    halves = list(half_products([packs[0]], [blocks[0]])) + halves
    vir_energy, halves[0] = lax.optimization_barrier((vir_energy, halves[0]))
    own_vir = lax.dynamic_slice_in_dim(vir_energy, me * rows, rows, 0)[:, None]
    dense, turned, scale, inverse = prepare(
        place, screen, pair_occ, occ_energy, blocks, metric, own_vir, vir_energy[None, :], tile
    )
    early = grids // 2
    mixed = mixed_sum(order[:early], place, turned, halves[:early])
    sent = ladders(order, order[early:], turned, scale, mixed, halves[early:])
    pieces = [exchange(sent[k], "grid", grids, k) if k else sent[k] for k in order]
    begun = result_start(order[:early], dense, pieces[:early])
    return results(order[early:], begun, dense, inverse, pieces[early:])[None]


def solution(mesh):
    in_specs = (
        P("pair", "grid", None),
        P(("grid", "pair"), None),
        P(),
        P(None, "grid"),
        P(),
        P(),
        P("pair", None),
    )
    return jax.shard_map(
        functools.partial(local, mesh.shape["grid"], mesh.shape["pair"]),
        mesh=mesh,
        in_specs=in_specs,
        out_specs=P("pair", "grid", None),
        check_vma=False,
    )
```
